512 devices in a mesh: lat: 8 (over x, core), lon: 16 (over y, z_hi), mem: 4 (over z_lo).
Axes of the slice: x: 4, y: 8, z: 8 (z_hi: 2, z_lo: 4; z = z_hi * 4 + z_lo), core: 2. Of those that a mesh axis runs over, the one named last changes fastest.
Arguments:
- perturbations: bfloat16 [32, 512, 4096], P('mem', 'lat', 'lon'), may hold values from -6 to 6
- diffusivity: float32 [512, 4096], P('lat', 'lon'), may hold values from 0.19 to 0.249
- sea_mask: int32 [512, 4096], P('lat', 'lon'), may hold values from 0 to 1
- obs_owner: int32 [1048576, 1], P(('lat', 'lon', 'mem')), may hold values from 0 to 127; in each aligned block of 2048 rows (0 to 2047, 2048 to 4095, ...) at most 32 rows name the same one
- obs_cell: int32 [1048576], P(('lat', 'lon', 'mem')), may hold values from 0 to 16383
- obs_depart: float32 [1048576], P(('lat', 'lon', 'mem')), may hold values from -6 to 6
- obs_weight: float32 [1048576], P(('lat', 'lon', 'mem')), may hold values from 0.25 to 2
Outputs:
- increment: float32 [512, 4096], P('lat', 'lon')
- obs_residual: float32 [1048576], P(('lat', 'lon', 'mem'))
The draws below stay inside these ranges and needn't reach their ends.
Inputs may be any that keep to these rules, and one draw needn't show every extreme that they name: `obs_owner`: within each device's aligned block of 2048 rows no tile is named by more than 32 rows, a bound that some block reaches.
All inputs are finite; a program needn't handle non-finite values.
Results may differ from the reference program's by a relative error of at most 0.0003.
Values sent between devices are 32-bit elements; how exact they have to be, the bound alone decides.
No kernel may reach another device: no remote copies, remote signals or barrier semaphores. Data moves between devices by JAX's collectives and lax.ppermute only.
A program may use at most 64 MiB of HBM per device.

```python
import math
import jax
import jax.numpy as jnp
import numpy as np
from jax import lax

LAT_DEV = 64
LON_DEV = 256
STEPS = 4
OBS_DEV = 2048
NLAT = 512
NLON = 4096
MEMBERS = 32
OWNERS = 128
CAP = 32
OBS = 1048576


def draw_sea_mask(key, part):
    key = jax.random.fold_in(key, 11)
    grid_rows = jnp.arange(NLAT, dtype=jnp.int32) % LAT_DEV
    grid_cols = jnp.arange(NLON, dtype=jnp.int32) % LON_DEV
    edge_rows = jnp.minimum(grid_rows, LAT_DEV - 1 - grid_rows) < 4
    edge_cols = jnp.minimum(grid_cols, LON_DEV - 1 - grid_cols) < 4
    border = edge_rows[:, None] | edge_cols[None, :]
    dice_values = jax.random.randint(key, (NLAT, NLON), 0, 320, dtype=jnp.int32)
    threshold = jnp.where(border, 5, 64).astype(jnp.int32)
    return jnp.where(dice_values < threshold, 0, 1).astype(jnp.int32)


def place_ends(drawn, own_key, smallest, largest):
    extent = drawn.shape
    spot = [jax.random.randint(jax.random.fold_in(own_key, axis), (), 0, extent[axis]) for axis in range(len(extent))]
    drawn = drawn.at[tuple(spot)].set(smallest)
    longest = extent.index(max(extent))
    spot[longest] = (spot[longest] + 1) % extent[longest]
    return drawn.at[tuple(spot)].set(largest)


def steps_of(key, extent, cuts, least, largest):
    def one(axis_at, shards_of):
        heights = jax.random.uniform(jax.random.fold_in(jax.random.fold_in(key, 6), axis_at), (shards_of,), jnp.float32, least / len(cuts), largest / len(cuts))
        return jnp.repeat(jnp.exp(heights), extent[axis_at] // shards_of).reshape((-1,) + (1,) * (len(extent) - axis_at - 1))

    loudness = one(*cuts[0])
    for cut in cuts[1:]:
        loudness = loudness * one(*cut)
    return loudness


def routed_block(stream_key, own, number, rows, amount, top, reach, skew):
    sequence = jax.random.permutation(stream_key, amount)
    crowded, ordinary = load_shares(amount, rows * top, reach, skew, True), load_shares(amount, rows * top, reach, skew, False)
    places = jnp.arange(amount)

    def named(lengths, turn):
        used = int((lengths > 0).sum())
        fixed = max(1, used // 4)
        moved = fixed + (places - fixed + turn * (used - fixed)) % max(1, amount - fixed)
        return jnp.zeros((amount,), jnp.int32).at[sequence[jnp.where(places < fixed, places, moved)]].set(jnp.asarray(lengths, jnp.int32))

    lengths = jnp.where(number % 4 == 0, named(crowded, number // 4), named(ordinary, number - number // 4 - 1))
    mixed = jax.random.permutation(jax.random.fold_in(own, 3), amount)
    donor, taker = mixed[0:amount // 2 * 2:2], mixed[1:amount // 2 * 2:2]
    margin = jnp.minimum(lengths[donor] - 1, reach - lengths[taker]) // 2
    margin = jnp.where((donor == sequence[0]) | (taker == sequence[0]) | (lengths[taker] == 0), 0, jnp.maximum(margin, 0))
    moved = jax.random.randint(jax.random.fold_in(own, 4), (amount // 2,), 0, 1 << 20) % (margin + 1)
    lengths = lengths.at[donor].add(-moved).at[taker].add(moved)
    labels = jnp.searchsorted(jnp.cumsum(lengths), jnp.arange(rows * top), side="right").astype(jnp.int32)
    table = labels.reshape(top, rows).T
    table = table[jax.random.permutation(jax.random.fold_in(own, 1), rows)]
    turn = jax.random.randint(jax.random.fold_in(own, 2), (rows, 1), 0, top)
    return jnp.take_along_axis(table, (jnp.arange(top)[None, :] + turn) % top, axis=1)


def load_shares(number_of, total, most, slope, full):
    weights = [(1 << 20) // math.isqrt(grade ** slope) + 1 for grade in range(1, number_of + 1)]
    largest = most if full else min(most, max(-(-total // number_of), total * weights[0] // sum(weights)))
    least = 1 if total - largest >= number_of - 1 else 0
    counts, surplus = [largest] + [least] * (number_of - 1), total - largest - least * (number_of - 1)
    while surplus > 0:
        free = [i for i in range(1, number_of) if counts[i] < largest] or [i for i in range(1, number_of) if counts[i] < most]
        whole, left = sum([weights[i] for i in free]), surplus
        for i in free:
            addition = min(most - counts[i], max(1, left * weights[i] // whole), surplus)
            counts[i] = counts[i] + addition
            surplus = surplus - addition
    return np.array(counts)


def centred(key, shape, scale, bound, pieces=(), kind=jnp.bfloat16):
    factor_of = steps_of(key, shape, pieces, -0.22, 0.18) if pieces else 1.0
    drawn = jax.random.normal(key, shape, jnp.float32) * scale * factor_of
    return jnp.minimum(jnp.maximum(drawn, -bound), bound).astype(kind)


def setup_inputs(seed: int = 0) -> dict:
    arg_keys = jax.random.split(jax.random.key(seed), 8)
    perturbations = centred(arg_keys[0], (MEMBERS, NLAT, NLON), 1.0, 6.0, ((0, 4), (1, 8), (2, 16)))
    diffusivity = jnp.clip(0.19 + 0.059 * jax.random.uniform(arg_keys[1], (NLAT, NLON), jnp.float32) ** steps_of(arg_keys[1], (NLAT, NLON), ((0, 8), (1, 16)), -0.2, 0.2), 0.19, 0.249)
    sea_mask = draw_sea_mask(jax.random.fold_in(arg_keys[7], 71), 0)
    obs_owner_keys = jax.random.split(jax.random.fold_in(arg_keys[3], 1), OBS // OBS_DEV)
    obs_owner_turns = jax.random.permutation(jax.random.fold_in(arg_keys[3], 3), OBS // OBS_DEV)
    obs_owner = jax.vmap(lambda own, number: routed_block(jax.random.fold_in(arg_keys[3], 2), own, number, OBS_DEV, OWNERS, 1, CAP, 2))(obs_owner_keys, obs_owner_turns).reshape((OBS, 1))
    obs_cell = place_ends(jax.random.randint(arg_keys[4], (OBS,), 0, LAT_DEV * LON_DEV), jax.random.fold_in(arg_keys[4], 1), 0, (LAT_DEV * LON_DEV) - 1).astype(jnp.int32)
    obs_depart = centred(arg_keys[5], (OBS,), 1.0, 6.0, ((0, 512),), jnp.float32)
    obs_weight = jnp.clip(jnp.exp(math.log(2.0) - 2.0794415 * jax.random.uniform(arg_keys[6], (OBS,), jnp.float32) ** steps_of(arg_keys[6], (OBS,), ((0, 512),), -0.2, 0.2)), 0.25, 2.0)
    return dict(perturbations=perturbations, diffusivity=diffusivity, sea_mask=sea_mask, obs_owner=obs_owner, obs_cell=obs_cell, obs_depart=obs_depart, obs_weight=obs_weight)


def diffuse_once(spread, north_face, east_face):
    flux_north = north_face * (spread[1:] - spread[:-1])
    zero_row = jnp.zeros((1, spread.shape[1]), spread.dtype)
    vertical = jnp.concatenate([flux_north, zero_row], 0) - jnp.concatenate([zero_row, flux_north], 0)
    flux_east = east_face * (jnp.roll(spread, -1, axis=1) - spread)
    return spread + vertical + (flux_east - jnp.roll(flux_east, 1, axis=1))


def covariance(source, perturbations, north_face, east_face, sea_cover):
    def add_member(summed, member):
        member_values = member.astype(jnp.float32)
        spread = member_values * source
        for sweep_index in range(STEPS):
            spread = diffuse_once(spread, north_face, east_face)
        return summed + member_values * spread, None

    summed, unused = lax.scan(add_member, jnp.zeros_like(source), perturbations)
    return sea_cover * summed / (MEMBERS - 1)


def reference(perturbations, diffusivity, sea_mask, obs_owner, obs_cell, obs_depart, obs_weight):
    sea_cover = sea_mask.astype(jnp.float32)
    north_face = 0.5 * (diffusivity[:-1] + diffusivity[1:]) * sea_cover[:-1] * sea_cover[1:]
    rate_next = jnp.roll(diffusivity, -1, axis=1)
    sea_next = jnp.roll(sea_cover, -1, axis=1)
    east_face = 0.5 * (diffusivity + rate_next) * sea_cover * sea_next
    tiles_lon = NLON // LON_DEV
    obs_dest = obs_owner[:, 0]
    grid_row = (obs_dest // tiles_lon) * LAT_DEV + obs_cell // LON_DEV
    grid_col = (obs_dest % tiles_lon) * LON_DEV + obs_cell % LON_DEV
    flat_cell = (grid_row * NLON + grid_col).astype(jnp.int32)
    tile_cells = NLAT * NLON
    innovation = jax.ops.segment_sum(obs_weight * obs_depart, flat_cell, num_segments=tile_cells).reshape(NLAT, NLON)
    first_pass = covariance(innovation, perturbations, north_face, east_face, sea_cover)
    at_obs = first_pass.reshape(-1)[flat_cell]
    removed = jax.ops.segment_sum(obs_weight * at_obs, flat_cell, num_segments=tile_cells).reshape(NLAT, NLON)
    corrected = innovation - removed
    increment = covariance(corrected, perturbations, north_face, east_face, sea_cover)
    obs_residual = obs_depart - increment.reshape(-1)[flat_cell]
    return increment, obs_residual
```

```python
import jax
import jax.numpy as jnp
from jax import lax
from jax.experimental import pallas as pl
from jax.experimental.pallas import tpu as pltpu
from jax.sharding import PartitionSpec as P

STEPS = 4
SLOTS = 32
HALO = 2 * STEPS
LANES = 128
F32 = jnp.float32
BF16 = jnp.bfloat16
I32 = jnp.int32

WHOLE = pl.BlockSpec(memory_space=pltpu.VMEM)


def call(kernel, outs, scratch=(), limit=24 << 20):
    def run(*operands):
        return pl.pallas_call(
            kernel,
            out_shape=outs,
            in_specs=[WHOLE] * len(operands),
            out_specs=jax.tree.map(lambda _: WHOLE, outs),
            scratch_shapes=list(scratch),
            compiler_params=pltpu.CompilerParams(vmem_limit_bytes=limit),
        )(*operands)

    return run


def halves(value):
    high = value.astype(BF16).astype(F32)
    return high, value - high


def nt_dot(a, b):
    return lax.dot_general(a, b, (((1,), (1,)), ((), ())), preferred_element_type=F32)


def pack_kernel(owner_ref, cell_ref, depart_ref, weight_ref, out_ref, rank_ref):
    places = out_ref.shape[0]
    chunks = owner_ref.shape[0]
    dest_ids = lax.broadcasted_iota(I32, (places, LANES), 0)
    slot_ids = lax.broadcasted_iota(I32, (SLOTS, LANES), 0).astype(F32)
    source = lax.broadcasted_iota(I32, (LANES, 2 * LANES), 0)
    target = lax.broadcasted_iota(I32, (LANES, 2 * LANES), 1)
    counter = jnp.where(source <= target, 1.0, 0.0).astype(BF16)
    seen = jnp.full((places, LANES), -1.0, F32)
    packed = jnp.zeros((places, 6 * SLOTS), F32)
    for j in range(chunks):
        hit = dest_ids == owner_ref[j : j + 1, :]
        names = jnp.where(hit, 1.0, 0.0).astype(BF16)
        counts = jnp.dot(names, counter, preferred_element_type=F32)
        rank = jnp.sum(jnp.where(hit, counts[:, :LANES] + seen, 0.0), axis=0, keepdims=True)
        seen = seen + counts[:, LANES:]
        rank_ref[j : j + 1, :] = rank
        weight = weight_ref[j : j + 1, :]
        product_high, product_low = halves(weight * depart_ref[j : j + 1, :])
        weight_high, weight_low = halves(weight)
        cell = cell_ref[j : j + 1, :]
        row = (cell // 256).astype(F32)
        col = (cell % 256).astype(F32)
        chosen = slot_ids == rank
        fields = [
            jnp.where(chosen, field, 0.0)
            for field in (product_high, weight_high, row, col, product_low, weight_low)
        ]
        packed = packed + nt_dot(names, jnp.concatenate(fields, axis=0).astype(BF16))
    low = jnp.concatenate(
        [packed[:, 4 * SLOTS :], jnp.zeros((places, 2 * SLOTS), F32)], axis=1
    )
    out_ref[...] = packed[:, : 4 * SLOTS] + low


def scatter_kernel(got_ref, out_ref, turned_ref):
    rows, cols = 64, 256
    turned_ref[...] = got_ref[...].T
    width = turned_ref.shape[1]
    row_ids = lax.broadcasted_iota(I32, (rows, width), 0).astype(F32)
    col_ids = lax.broadcasted_iota(I32, (cols, width), 0).astype(F32)
    total = jnp.zeros((4 * rows, cols), F32)
    for s in range(0, SLOTS, 2):
        left, right = [], []
        for k in (s, s + 1):
            product_high, product_low = halves(turned_ref[k : k + 1, :])
            weight_high, weight_low = halves(turned_ref[SLOTS + k : SLOTS + k + 1, :])
            in_row = row_ids == turned_ref[2 * SLOTS + k : 2 * SLOTS + k + 1, :]
            in_col = col_ids == turned_ref[3 * SLOTS + k : 3 * SLOTS + k + 1, :]
            left.append(
                jnp.concatenate(
                    [
                        jnp.where(in_row, v, 0.0)
                        for v in (product_high, product_low, weight_high, weight_low)
                    ],
                    axis=0,
                ).astype(BF16)
            )
            right.append(jnp.where(in_col, 1.0, 0.0).astype(BF16))
        total = total + nt_dot(jnp.concatenate(left, axis=1), jnp.concatenate(right, axis=1))
    product = total[:rows] + total[rows : 2 * rows]
    weight = total[2 * rows : 3 * rows] + total[3 * rows :]
    quarters, width = out_ref.shape[0], out_ref.shape[2] // 2
    for q in range(quarters):
        out_ref[q, :, :width] = product[:, q * width : (q + 1) * width]
        out_ref[q, :, width:] = weight[:, q * width : (q + 1) * width]


def reduce_kernel(parts_ref, whole_ref, top_ref, bottom_ref):
    whole = parts_ref[0]
    for q in range(1, parts_ref.shape[0]):
        whole = whole + parts_ref[q]
    whole_ref[...] = whole
    top_ref[...] = whole[:HALO]
    bottom_ref[...] = whole[-HALO:]


def rim_kernel(north_ref, whole_ref, south_ref, out_ref):
    out_ref[:HALO] = north_ref[...]
    out_ref[HALO:-HALO] = whole_ref[...]
    out_ref[-HALO:] = south_ref[...]


def row_rim_kernel(members_ref, rate_ref, sea_ref, top_ref, bottom_ref):
    members, rows, _ = members_ref.shape
    for k in range(members):
        value = members_ref[k].astype(F32)
        top_ref[k] = value[:HALO]
        bottom_ref[k] = value[rows - HALO :]
    top_ref[members] = rate_ref[:HALO]
    bottom_ref[members] = rate_ref[rows - HALO :]
    top_ref[members + 1] = sea_ref[:HALO].astype(F32)
    bottom_ref[members + 1] = sea_ref[rows - HALO :].astype(F32)


def field_of(k, members_ref, rate_ref, sea_ref):
    members = members_ref.shape[0]
    if k < members:
        return members_ref[k].astype(F32)
    return rate_ref[...] if k == members else sea_ref[...].astype(F32)


def col_rim_kernel(members_ref, rate_ref, sea_ref, north_ref, south_ref, first_ref, last_ref):
    fields = members_ref.shape[0] + 2
    rows, cols = rate_ref.shape
    first_ref[...] = jnp.zeros(first_ref.shape, F32)
    last_ref[...] = jnp.zeros(last_ref.shape, F32)
    for k in range(fields):
        value = field_of(k, members_ref, rate_ref, sea_ref)
        at = slice(k * HALO, (k + 1) * HALO)
        for ref, cut in ((first_ref, slice(0, HALO)), (last_ref, slice(cols - HALO, cols))):
            ref[:HALO, at] = north_ref[k, :, cut]
            ref[HALO : HALO + rows, at] = value[:, cut]
            ref[HALO + rows :, at] = south_ref[k, :, cut]


def piece_kernel(
    members_ref, rate_ref, sea_ref, north_ref, south_ref, west_ref, east_ref,
    pieces_ref, coef_ref, wide_ref, kept_ref,
):
    members = members_ref.shape[0]
    rows, cols = rate_ref.shape
    quarters = pieces_ref.shape[0]
    width = cols // quarters
    span = width + 2 * HALO
    for k in range(members + 2):
        value = field_of(k, members_ref, rate_ref, sea_ref)
        at = slice(k * HALO, (k + 1) * HALO)
        wide_ref[:, :HALO] = west_ref[:, at]
        wide_ref[:HALO, HALO : HALO + cols] = north_ref[k]
        wide_ref[HALO : HALO + rows, HALO : HALO + cols] = value
        wide_ref[HALO + rows :, HALO : HALO + cols] = south_ref[k]
        wide_ref[:, HALO + cols : 2 * HALO + cols] = east_ref[:, at]
        for q in range(quarters):
            piece = wide_ref[:, q * width : q * width + span]
            if k < members:
                pieces_ref[q, :, k * span : (k + 1) * span] = piece
            else:
                kept_ref[q, k - members, :, :span] = piece
    mine = lax.axis_index("mem")
    lat, last = lax.axis_index("lat"), lax.axis_size("lat") - 1
    coef_ref[0] = kept_ref[mine, 0]
    row_ids = lax.broadcasted_iota(I32, (rows + 2 * HALO, coef_ref.shape[2]), 0)
    outside = ((row_ids < HALO) & (lat == 0)) | ((row_ids >= HALO + rows) & (lat == last))
    coef_ref[1] = jnp.where(outside, 0.0, kept_ref[mine, 1])


def product_kernel(
    own_ref, west_ref, east_ref, members_ref, coef_ref, out_ref,
    state_ref, weights_ref, tiled_ref, field_ref,
):
    groups, height, lanes = members_ref.shape
    width = own_ref.shape[1] // 2
    span = width + 2 * HALO
    windows = lanes // span
    divisor = groups * windows - 1
    pad = 8

    def tile_lanes(value):
        for k in range(windows):
            tiled_ref[:, k * span : (k + 1) * span] = value
        return tiled_ref[...]

    for f in range(2):
        low = f * width
        field_ref[f, :, :HALO] = west_ref[:, low + width - HALO : low + width]
        field_ref[f, :, HALO : HALO + width] = own_ref[:, low : low + width]
        field_ref[f, :, HALO + width : span] = east_ref[:, low : low + HALO]
    innovation = field_ref[0, :, :span]
    weight_sum = field_ref[1, :, :span]
    sea_cover = coef_ref[1, :, :span]

    rate = tile_lanes(coef_ref[0, :, :span])
    sea = tile_lanes(sea_cover)
    north = 0.5 * (rate + pltpu.roll(rate, height - 1, 0)) * sea * pltpu.roll(sea, height - 1, 0)
    east = 0.5 * (rate + pltpu.roll(rate, lanes - 1, 1)) * sea * pltpu.roll(sea, lanes - 1, 1)
    south = pltpu.roll(north, 1, 0)
    west = pltpu.roll(east, 1, 1)
    weights_ref[0] = 1.0 - (north + south + east + west)
    weights_ref[1] = north
    weights_ref[2] = south
    weights_ref[3] = east
    weights_ref[4] = west
    state_ref[...] = jnp.zeros(state_ref.shape, F32)

    def sweep(source, target):
        for r in range(0, height, 8):
            centre_w, north_w, south_w, east_w, west_w = (
                weights_ref[i, r : r + 8, :] for i in range(5)
            )
            for g in range(groups):
                centre = state_ref[source, g, pad + r : pad + r + 8, :]
                above = state_ref[source, g, pad + r + 1 : pad + r + 9, :]
                below = state_ref[source, g, pad + r - 1 : pad + r + 7, :]
                state_ref[target, g, pad + r : pad + r + 8, :] = (
                    centre_w * centre
                    + (north_w * above + south_w * below)
                    + (east_w * pltpu.roll(centre, lanes - 1, 1) + west_w * pltpu.roll(centre, 1, 1))
                )

    def covariance(source):
        tiled = tile_lanes(source)
        for g in range(groups):
            state_ref[0, g, pad : pad + height, :] = members_ref[g] * tiled

        def pair(_, carry):
            sweep(0, 1)
            sweep(1, 0)
            return carry

        lax.fori_loop(0, STEPS // 2, pair, 0)
        total = members_ref[0] * state_ref[0, 0, pad : pad + height, :]
        for g in range(1, groups):
            total = total + members_ref[g] * state_ref[0, g, pad : pad + height, :]
        tiled_ref[...] = total
        summed = tiled_ref[:, :span]
        for k in range(1, windows):
            summed = summed + tiled_ref[:, k * span : (k + 1) * span]
        return sea_cover * summed / divisor

    first_pass = covariance(innovation)
    increment = covariance(innovation - weight_sum * first_pass)
    field_ref[0, :, :span] = increment
    half = (height - 2 * HALO) // 2
    for q in range(out_ref.shape[0]):
        out_ref[q, :, :width] = field_ref[0, HALO : HALO + half, HALO : HALO + width]
        out_ref[q, :, width:] = field_ref[0, HALO + half : HALO + 2 * half, HALO : HALO + width]


def answer_kernel(pieces_ref, turned_ref, tile_ref, out_ref, reply_ref):
    quarters, half, width = pieces_ref.shape[0], pieces_ref.shape[1], pieces_ref.shape[2] // 2
    rows, cols = tile_ref.shape
    for q in range(quarters):
        tile_ref[:half, q * width : (q + 1) * width] = pieces_ref[q, :, :width]
        tile_ref[half:, q * width : (q + 1) * width] = pieces_ref[q, :, width:]
    high, low = halves(tile_ref[...])
    both = jnp.concatenate([high, low], axis=0).astype(BF16)
    lanes = turned_ref.shape[1]
    row_ids = lax.broadcasted_iota(I32, (rows, lanes), 0).astype(F32)
    col_ids = lax.broadcasted_iota(I32, (cols, lanes), 0).astype(F32)
    reply_ref[...] = jnp.zeros(reply_ref.shape, F32)
    for k in range(SLOTS):
        in_row = row_ids == turned_ref[2 * SLOTS + k : 2 * SLOTS + k + 1, :]
        in_col = col_ids == turned_ref[3 * SLOTS + k : 3 * SLOTS + k + 1, :]
        picked = jnp.dot(both, jnp.where(in_col, 1.0, 0.0).astype(BF16), preferred_element_type=F32)
        picked = picked[:rows] + picked[rows:]
        reply_ref[k : k + 1, :] = jnp.sum(jnp.where(in_row, picked, 0.0), axis=0, keepdims=True)
    out_ref[...] = reply_ref[...].T[:, :SLOTS]


def residual_kernel(owner_ref, rank_ref, depart_ref, got_ref, out_ref, wide_ref):
    places = got_ref.shape[0]
    chunks = owner_ref.shape[0]
    wide_ref[...] = jnp.zeros(wide_ref.shape, F32)
    wide_ref[:places, :SLOTS] = got_ref[...]
    turned = wide_ref[...].T[:SLOTS, :]
    high, low = halves(turned)
    both = jnp.concatenate([high, low], axis=0).astype(BF16)
    dest_ids = lax.broadcasted_iota(I32, (wide_ref.shape[0], LANES), 0)
    slot_ids = lax.broadcasted_iota(I32, (SLOTS, LANES), 0).astype(F32)
    for j in range(chunks):
        names = jnp.where(dest_ids == owner_ref[j : j + 1, :], 1.0, 0.0).astype(BF16)
        picked = jnp.dot(both, names, preferred_element_type=F32)
        picked = picked[:SLOTS] + picked[SLOTS:]
        value = jnp.sum(
            jnp.where(slot_ids == rank_ref[j : j + 1, :], picked, 0.0), axis=0, keepdims=True
        )
        out_ref[j : j + 1, :] = depart_ref[j : j + 1, :] - value


def shape(*dims, dtype=F32):
    return jax.ShapeDtypeStruct(dims, dtype)


def neighbours(axes):
    size = 1
    for axis in axes:
        size *= lax.axis_size(axis)
    up = [(i, (i + 1) % size) for i in range(size)]
    return up, [(j, i) for i, j in up]


def exchange(first, last, axes):
    up, down = neighbours(axes)
    return lax.ppermute(last, axes, up), lax.ppermute(first, axes, down)


def per_device(perturbations, diffusivity, sea_mask, obs_owner, obs_cell, obs_depart, obs_weight):
    members, rows, cols = perturbations.shape
    quarters = lax.axis_size("mem")
    places = lax.axis_size("lat") * lax.axis_size("lon")
    width = cols // quarters
    span = width + 2 * HALO
    height = rows + 2 * HALO
    chunks = obs_cell.shape[0] // LANES
    owner, cell, depart, weight = (
        a.reshape(chunks, LANES) for a in (obs_owner, obs_cell, obs_depart, obs_weight)
    )
    tiles = ("lat", "lon")

    top, bottom = call(
        row_rim_kernel, (shape(members + 2, HALO, cols), shape(members + 2, HALO, cols))
    )(perturbations, diffusivity, sea_mask)
    north, south = exchange(top, bottom, ("lat",))
    outgoing, rank = call(pack_kernel, (shape(places, LANES), shape(chunks, LANES)))(
        owner, cell, depart, weight
    )
    got = lax.all_to_all(outgoing, tiles, split_axis=0, concat_axis=0, tiled=True)

    first, last = call(col_rim_kernel, (shape(height, LANES), shape(height, LANES)))(
        perturbations, diffusivity, sea_mask, north, south
    )
    west, east = exchange(first, last, ("lon",))
    pieces, coef = call(
        piece_kernel,
        (shape(quarters, height, members * span), shape(2, height, LANES)),
        [pltpu.VMEM((height, cols + LANES), F32), pltpu.VMEM((quarters, 2, height, LANES), F32)],
    )(perturbations, diffusivity, sea_mask, north, south, west, east)
    all_members = lax.all_to_all(pieces, "mem", split_axis=0, concat_axis=0, tiled=True)

    parts, turned = call(
        scatter_kernel, (shape(quarters, rows, 2 * width), shape(LANES, places))
    )(got)
    parts = lax.all_to_all(parts, "mem", split_axis=0, concat_axis=0, tiled=True)
    whole, top, bottom = call(
        reduce_kernel,
        (shape(rows, 2 * width), shape(HALO, 2 * width), shape(HALO, 2 * width)),
    )(parts)
    north, south = exchange(top, bottom, ("lat",))
    own = call(rim_kernel, shape(height, 2 * width))(north, whole, south)
    west, east = exchange(own, own, ("lon", "mem"))
    lanes = members * span
    quarter = call(
        product_kernel,
        shape(quarters, rows // 2, 2 * width),
        [
            pltpu.VMEM((2, quarters, height + 16, lanes), F32),
            pltpu.VMEM((5, height, lanes), F32),
            pltpu.VMEM((height, lanes), F32),
            pltpu.VMEM((2, height, LANES), F32),
        ],
    )(own, west, east, all_members, coef)
    quarter = lax.all_to_all(quarter, "mem", split_axis=0, concat_axis=0, tiled=True)
    increment, answers = call(
        answer_kernel, (shape(rows, cols), shape(places, SLOTS)), [pltpu.VMEM((LANES, places), F32)]
    )(quarter, turned)
    returned = lax.all_to_all(answers, tiles, split_axis=0, concat_axis=0, tiled=True)
    residual = call(
        residual_kernel, shape(chunks, LANES), [pltpu.VMEM((max(LANES, places), LANES), F32)]
    )(owner, rank, depart, returned)
    return increment, residual.reshape(chunks * LANES)


def solution(mesh):
    return jax.shard_map(
        per_device,
        mesh=mesh,
        in_specs=(
            P("mem", "lat", "lon"),
            P("lat", "lon"),
            P("lat", "lon"),
            P(("lat", "lon", "mem"), None),
            P(("lat", "lon", "mem")),
            P(("lat", "lon", "mem")),
            P(("lat", "lon", "mem")),
        ),
        out_specs=(P("lat", "lon"), P(("lat", "lon", "mem"))),
        check_vma=False,
    )
```

```python
import functools

import jax
import jax.numpy as jnp
from jax import lax
from jax.experimental import pallas as pl
from jax.experimental.pallas import tpu as pltpu
from jax.sharding import PartitionSpec as P

STEPS = 4
SLOTS = 32
HALO = 2 * STEPS
LANES = 128
F32 = jnp.float32
BF16 = jnp.bfloat16
I32 = jnp.int32

WHOLE = pl.BlockSpec(memory_space=pltpu.VMEM)
AWAY = pl.BlockSpec(memory_space=pl.ANY)


def call(kernel, outs, scratch=(), limit=24 << 20, place=WHOLE):
    def run(*operands):
        return pl.pallas_call(
            kernel,
            out_shape=outs,
            in_specs=[place] * len(operands),
            out_specs=jax.tree.map(lambda _: WHOLE, outs),
            scratch_shapes=list(scratch),
            compiler_params=pltpu.CompilerParams(vmem_limit_bytes=limit),
        )(*operands)

    return run


def halves(value):
    high = value.astype(BF16).astype(F32)
    return high, value - high


def nt_dot(a, b):
    return lax.dot_general(a, b, (((1,), (1,)), ((), ())), preferred_element_type=F32)


def bring(away_refs, near_refs, sem_ref):
    copies = [
        pltpu.make_async_copy(away, near, sem_ref.at[i])
        for i, (away, near) in enumerate(zip(away_refs, near_refs))
    ]
    for copy in copies:
        copy.start()
    for copy in copies:
        copy.wait()


def pack_kernel(*refs):
    out_ref, rank_ref = refs[4:6]
    owner_ref, cell_ref, depart_ref, weight_ref = refs[6:10]
    bring(refs[:4], refs[6:10], refs[10])
    places = out_ref.shape[0]
    chunks = owner_ref.shape[0]
    dest_ids = lax.broadcasted_iota(I32, (places, LANES), 0)
    slot_ids = lax.broadcasted_iota(I32, (SLOTS, LANES), 0).astype(F32)
    source = lax.broadcasted_iota(I32, (LANES, 2 * LANES), 0)
    target = lax.broadcasted_iota(I32, (LANES, 2 * LANES), 1)
    counter = jnp.where(source <= target, 1.0, 0.0).astype(BF16)
    seen = jnp.full((places, LANES), -1.0, F32)
    packed = jnp.zeros((places, 6 * SLOTS), F32)
    for j in range(chunks):
        hit = dest_ids == owner_ref[j : j + 1, :]
        names = jnp.where(hit, 1.0, 0.0).astype(BF16)
        counts = jnp.dot(names, counter, preferred_element_type=F32)
        rank = jnp.sum(jnp.where(hit, counts[:, :LANES] + seen, 0.0), axis=0, keepdims=True)
        seen = seen + counts[:, LANES:]
        rank_ref[j : j + 1, :] = rank
        weight = weight_ref[j : j + 1, :]
        product_high, product_low = halves(weight * depart_ref[j : j + 1, :])
        weight_high, weight_low = halves(weight)
        cell = cell_ref[j : j + 1, :]
        row = (cell // 256).astype(F32)
        col = (cell % 256).astype(F32)
        chosen = slot_ids == rank
        fields = [
            jnp.where(chosen, field, 0.0)
            for field in (product_high, weight_high, row, col, product_low, weight_low)
        ]
        packed = packed + nt_dot(names, jnp.concatenate(fields, axis=0).astype(BF16))
    low = jnp.concatenate(
        [packed[:, 4 * SLOTS :], jnp.zeros((places, 2 * SLOTS), F32)], axis=1
    )
    out_ref[...] = packed[:, : 4 * SLOTS] + low


def scatter_kernel(got_ref, out_ref, turned_ref):
    rows, cols = 64, 256
    turned_ref[...] = got_ref[...].T
    width = turned_ref.shape[1]
    row_ids = lax.broadcasted_iota(I32, (rows, width), 0).astype(F32)
    col_ids = lax.broadcasted_iota(I32, (cols, width), 0).astype(F32)
    total = jnp.zeros((4 * rows, cols), F32)
    for s in range(0, SLOTS, 2):
        left, right = [], []
        for k in (s, s + 1):
            product_high, product_low = halves(turned_ref[k : k + 1, :])
            weight_high, weight_low = halves(turned_ref[SLOTS + k : SLOTS + k + 1, :])
            in_row = row_ids == turned_ref[2 * SLOTS + k : 2 * SLOTS + k + 1, :]
            in_col = col_ids == turned_ref[3 * SLOTS + k : 3 * SLOTS + k + 1, :]
            left.append(
                jnp.concatenate(
                    [
                        jnp.where(in_row, v, 0.0)
                        for v in (product_high, product_low, weight_high, weight_low)
                    ],
                    axis=0,
                ).astype(BF16)
            )
            right.append(jnp.where(in_col, 1.0, 0.0).astype(BF16))
        total = total + nt_dot(jnp.concatenate(left, axis=1), jnp.concatenate(right, axis=1))
    product = total[:rows] + total[rows : 2 * rows]
    weight = total[2 * rows : 3 * rows] + total[3 * rows :]
    quarters, width = out_ref.shape[0], out_ref.shape[2] // 2
    for q in range(quarters):
        out_ref[q, :, :width] = product[:, q * width : (q + 1) * width]
        out_ref[q, :, width:] = weight[:, q * width : (q + 1) * width]


def quarter_kernel(members_ref, own_ref, *rest):
    sent_refs, kept_ref = rest[:-1], rest[-1]
    members = members_ref.shape[0]
    quarters = kept_ref.shape[0]
    width = members_ref.shape[2] // quarters
    for k in range(members):
        value = members_ref[k].astype(F32)
        for q in range(quarters):
            kept_ref[q, :, k * width : (k + 1) * width] = value[:, q * width : (q + 1) * width]
    mine = lax.axis_index("mem")
    own_ref[...] = kept_ref[mine]
    for k, ref in enumerate(sent_refs):
        ref[...] = kept_ref[(mine + k + 1) % quarters]


def reduce_kernel(parts_ref, rate_ref, sea_ref, *rest):
    quarters = parts_ref.shape[0]
    piece_refs, (mid_ref, top_ref, bottom_ref, kept_ref) = rest[:quarters], rest[quarters:]
    rows, lanes = piece_refs[0].shape
    width = parts_ref.shape[2] // 2
    mine = lax.axis_index("mem")
    for k in range(quarters):
        mid_ref[(mine - k + quarters) % quarters, :, :lanes] = piece_refs[k][...]
    whole = parts_ref[0]
    for q in range(1, quarters):
        whole = whole + parts_ref[q]
    mid_ref[0, :, lanes:] = whole
    for q in range(quarters):
        at = slice(q * width, (q + 1) * width)
        kept_ref[q, :, :width] = rate_ref[:, at]
        kept_ref[q, :, width:] = sea_ref[:, at].astype(F32)
    mid_ref[1, :, lanes:] = kept_ref[mine]
    for q in range(quarters):
        size = lanes if q > 1 else lanes + 2 * width
        top_ref[q, :, :size] = mid_ref[q, :HALO, :size]
        bottom_ref[q, :, :size] = mid_ref[q, rows - HALO :, :size]
        if size < top_ref.shape[2]:
            top_ref[q, :, size:] = jnp.zeros((HALO, 2 * width), F32)
            bottom_ref[q, :, size:] = jnp.zeros((HALO, 2 * width), F32)


def fields_of(ref, width):
    quarters, lanes = ref.shape[0], ref.shape[2] - 2 * width
    places = [(q, k * width) for q in range(quarters) for k in range(lanes // width)]
    return places + [(0, lanes), (0, lanes + width), (1, lanes), (1, lanes + width)]


def outside_rows(rows):
    lat = lax.axis_index("lat")
    return lat == 0, lat == lax.axis_size("lat") - 1


def rim_kernel(mid_ref, north_ref, south_ref, first_ref, last_ref, *, width):
    rows = mid_ref.shape[1]
    first_ref[...] = jnp.zeros(first_ref.shape, F32)
    last_ref[...] = jnp.zeros(last_ref.shape, F32)
    places = fields_of(mid_ref, width)
    no_north, no_south = outside_rows(rows)
    for k, (q, lane) in enumerate(places):
        at = slice(k * HALO, (k + 1) * HALO)
        for ref, cut in ((first_ref, lane), (last_ref, lane + width - HALO)):
            north = north_ref[q, :, cut : cut + HALO]
            south = south_ref[q, :, cut : cut + HALO]
            if k == len(places) - 1:
                north = jnp.where(no_north, 0.0, north)
                south = jnp.where(no_south, 0.0, south)
            ref[:HALO, at] = north
            ref[HALO : HALO + rows, at] = mid_ref[q, :, cut : cut + HALO]
            ref[HALO + rows :, at] = south


def product_kernel(
    mid_ref, north_ref, south_ref, west_ref, east_ref, out_ref,
    members_ref, state_ref, weights_ref, tiled_ref, field_ref,
):
    groups, height, lanes = members_ref.shape
    rows = height - 2 * HALO
    width = out_ref.shape[2] // 2
    span = width + 2 * HALO
    windows = lanes // span
    divisor = groups * windows - 1
    pad = 8

    def tile_lanes(value):
        for k in range(windows):
            tiled_ref[:, k * span : (k + 1) * span] = value
        return tiled_ref[...]

    places = fields_of(mid_ref, width)
    no_north, no_south = outside_rows(rows)
    for k, (q, lane) in enumerate(places):
        rim = slice(k * HALO, (k + 1) * HALO)
        cut = slice(lane, lane + width)
        north, south = north_ref[q, :, cut], south_ref[q, :, cut]
        if k < groups * windows:
            ref, low = members_ref.at[k // windows], k % windows * span
        else:
            ref, low = field_ref.at[k - groups * windows], 0
        if k == len(places) - 1:
            north = jnp.where(no_north, 0.0, north)
            south = jnp.where(no_south, 0.0, south)
        ref[:, low : low + HALO] = west_ref[:, rim]
        ref[:HALO, low + HALO : low + HALO + width] = north
        ref[HALO : HALO + rows, low + HALO : low + HALO + width] = mid_ref[q, :, cut]
        ref[HALO + rows :, low + HALO : low + HALO + width] = south
        ref[:, low + HALO + width : low + span] = east_ref[:, rim]
    innovation = field_ref[0, :, :span]
    weight_sum = field_ref[1, :, :span]
    sea_cover = field_ref[3, :, :span]

    rate = tile_lanes(field_ref[2, :, :span])
    sea = tile_lanes(sea_cover)
    north = 0.5 * (rate + pltpu.roll(rate, height - 1, 0)) * sea * pltpu.roll(sea, height - 1, 0)
    east = 0.5 * (rate + pltpu.roll(rate, lanes - 1, 1)) * sea * pltpu.roll(sea, lanes - 1, 1)
    south = pltpu.roll(north, 1, 0)
    west = pltpu.roll(east, 1, 1)
    weights_ref[0] = 1.0 - (north + south + east + west)
    weights_ref[1] = north
    weights_ref[2] = south
    weights_ref[3] = east
    weights_ref[4] = west
    state_ref[...] = jnp.zeros(state_ref.shape, F32)

    def sweep(source, target):
        for r in range(0, height, 8):
            centre_w, north_w, south_w, east_w, west_w = (
                weights_ref[i, r : r + 8, :] for i in range(5)
            )
            for g in range(groups):
                centre = state_ref[source, g, pad + r : pad + r + 8, :]
                above = state_ref[source, g, pad + r + 1 : pad + r + 9, :]
                below = state_ref[source, g, pad + r - 1 : pad + r + 7, :]
                state_ref[target, g, pad + r : pad + r + 8, :] = (
                    centre_w * centre
                    + (north_w * above + south_w * below)
                    + (east_w * pltpu.roll(centre, lanes - 1, 1) + west_w * pltpu.roll(centre, 1, 1))
                )

    def covariance(source):
        tiled = tile_lanes(source)
        for g in range(groups):
            state_ref[0, g, pad : pad + height, :] = members_ref[g] * tiled

        def pair(_, carry):
            sweep(0, 1)
            sweep(1, 0)
            return carry

        lax.fori_loop(0, STEPS // 2, pair, 0)
        total = members_ref[0] * state_ref[0, 0, pad : pad + height, :]
        for g in range(1, groups):
            total = total + members_ref[g] * state_ref[0, g, pad : pad + height, :]
        tiled_ref[...] = total
        summed = tiled_ref[:, :span]
        for k in range(1, windows):
            summed = summed + tiled_ref[:, k * span : (k + 1) * span]
        return sea_cover * summed / divisor

    first_pass = covariance(innovation)
    increment = covariance(innovation - weight_sum * first_pass)
    field_ref[0, :, :span] = increment
    half = (height - 2 * HALO) // 2
    for q in range(out_ref.shape[0]):
        out_ref[q, :, :width] = field_ref[0, HALO : HALO + half, HALO : HALO + width]
        out_ref[q, :, width:] = field_ref[0, HALO + half : HALO + 2 * half, HALO : HALO + width]


def answer_kernel(pieces_ref, turned_ref, tile_ref, out_ref, reply_ref):
    quarters, half, width = pieces_ref.shape[0], pieces_ref.shape[1], pieces_ref.shape[2] // 2
    rows, cols = tile_ref.shape
    for q in range(quarters):
        tile_ref[:half, q * width : (q + 1) * width] = pieces_ref[q, :, :width]
        tile_ref[half:, q * width : (q + 1) * width] = pieces_ref[q, :, width:]
    high, low = halves(tile_ref[...])
    both = jnp.concatenate([high, low], axis=0).astype(BF16)
    lanes = turned_ref.shape[1]
    row_ids = lax.broadcasted_iota(I32, (rows, lanes), 0).astype(F32)
    col_ids = lax.broadcasted_iota(I32, (cols, lanes), 0).astype(F32)
    reply_ref[...] = jnp.zeros(reply_ref.shape, F32)
    for k in range(SLOTS):
        in_row = row_ids == turned_ref[2 * SLOTS + k : 2 * SLOTS + k + 1, :]
        in_col = col_ids == turned_ref[3 * SLOTS + k : 3 * SLOTS + k + 1, :]
        picked = jnp.dot(both, jnp.where(in_col, 1.0, 0.0).astype(BF16), preferred_element_type=F32)
        picked = picked[:rows] + picked[rows:]
        reply_ref[k : k + 1, :] = jnp.sum(jnp.where(in_row, picked, 0.0), axis=0, keepdims=True)
    out_ref[...] = reply_ref[...].T[:, :SLOTS]


def residual_kernel(owner_ref, rank_ref, depart_ref, got_ref, out_ref, wide_ref):
    places = got_ref.shape[0]
    chunks = owner_ref.shape[0]
    wide_ref[...] = jnp.zeros(wide_ref.shape, F32)
    wide_ref[:places, :SLOTS] = got_ref[...]
    turned = wide_ref[...].T[:SLOTS, :]
    high, low = halves(turned)
    both = jnp.concatenate([high, low], axis=0).astype(BF16)
    dest_ids = lax.broadcasted_iota(I32, (wide_ref.shape[0], LANES), 0)
    slot_ids = lax.broadcasted_iota(I32, (SLOTS, LANES), 0).astype(F32)
    for j in range(chunks):
        names = jnp.where(dest_ids == owner_ref[j : j + 1, :], 1.0, 0.0).astype(BF16)
        picked = jnp.dot(both, names, preferred_element_type=F32)
        picked = picked[:SLOTS] + picked[SLOTS:]
        value = jnp.sum(
            jnp.where(slot_ids == rank_ref[j : j + 1, :], picked, 0.0), axis=0, keepdims=True
        )
        out_ref[j : j + 1, :] = depart_ref[j : j + 1, :] - value


def shape(*dims, dtype=F32):
    return jax.ShapeDtypeStruct(dims, dtype)


def neighbours(axes):
    size = 1
    for axis in axes:
        size *= lax.axis_size(axis)
    up = [(i, (i + 1) % size) for i in range(size)]
    return up, [(j, i) for i, j in up]


def exchange(first, last, axes):
    up, down = neighbours(axes)
    return lax.ppermute(last, axes, up), lax.ppermute(first, axes, down)


def per_device(perturbations, diffusivity, sea_mask, obs_owner, obs_cell, obs_depart, obs_weight):
    members, rows, cols = perturbations.shape
    quarters = lax.axis_size("mem")
    places = lax.axis_size("lat") * lax.axis_size("lon")
    width = cols // quarters
    span = width + 2 * HALO
    height = rows + 2 * HALO
    chunks = obs_cell.shape[0] // LANES
    owner, cell, depart, weight = (
        a.reshape(chunks, LANES) for a in (obs_owner, obs_cell, obs_depart, obs_weight)
    )
    tiles = ("lat", "lon")

    piece = shape(rows, members * width)
    own, *sent = call(quarter_kernel, [piece] * quarters, [pltpu.VMEM((quarters, rows, members * width), F32)])(
        perturbations
    )
    ring = [
        [(i, (i + k) % quarters) for i in range(quarters)] for k in range(1, quarters)
    ]
    outgoing, rank = call(
        pack_kernel,
        (shape(places, LANES), shape(chunks, LANES)),
        [pltpu.VMEM((chunks, LANES), a.dtype) for a in (owner, cell, depart, weight)]
        + [pltpu.SemaphoreType.DMA((4,))],
        place=AWAY,
    )(owner, cell, depart, weight)
    got = lax.all_to_all(outgoing, tiles, split_axis=0, concat_axis=0, tiled=True)
    brought = [lax.ppermute(s, "mem", pairs) for s, pairs in zip(sent, ring)]
    got, *brought = lax.optimization_barrier((got, *brought))

    parts, turned = call(
        scatter_kernel, (shape(quarters, rows, 2 * width), shape(LANES, places))
    )(got)
    parts = lax.all_to_all(parts, "mem", split_axis=0, concat_axis=0, tiled=True)
    field_lanes = members * width + 2 * width
    strip = shape(quarters, HALO, field_lanes)
    mid, top, bottom = call(
        reduce_kernel,
        (shape(quarters, rows, field_lanes), strip, strip),
        [pltpu.VMEM((quarters, rows, 2 * width), F32)],
    )(parts, diffusivity, sea_mask, own, *brought)
    north, south = exchange(top, bottom, ("lat",))
    rim_lanes = -(-(quarters * members + 4) * HALO // LANES) * LANES
    rim = shape(height, rim_lanes)
    first, last = call(functools.partial(rim_kernel, width=width), (rim, rim))(mid, north, south)
    west, east = exchange(first, last, ("lon", "mem"))
    lanes = members * span
    quarter = call(
        product_kernel,
        shape(quarters, rows // 2, 2 * width),
        [
            pltpu.VMEM((quarters, height, lanes), F32),
            pltpu.VMEM((2, quarters, height + 16, lanes), F32),
            pltpu.VMEM((5, height, lanes), F32),
            pltpu.VMEM((height, lanes), F32),
            pltpu.VMEM((4, height, LANES), F32),
        ],
    )(mid, north, south, west, east)
    quarter = lax.all_to_all(quarter, "mem", split_axis=0, concat_axis=0, tiled=True)
    increment, answers = call(
        answer_kernel, (shape(rows, cols), shape(places, SLOTS)), [pltpu.VMEM((LANES, places), F32)]
    )(quarter, turned)
    returned = lax.all_to_all(answers, tiles, split_axis=0, concat_axis=0, tiled=True)
    residual = call(
        residual_kernel, shape(chunks, LANES), [pltpu.VMEM((max(LANES, places), LANES), F32)]
    )(owner, rank, depart, returned)
    return increment, residual.reshape(chunks * LANES)


def solution(mesh):
    return jax.shard_map(
        per_device,
        mesh=mesh,
        in_specs=(
            P("mem", "lat", "lon"),
            P("lat", "lon"),
            P("lat", "lon"),
            P(("lat", "lon", "mem"), None),
            P(("lat", "lon", "mem")),
            P(("lat", "lon", "mem")),
            P(("lat", "lon", "mem")),
        ),
        out_specs=(P("lat", "lon"), P(("lat", "lon", "mem"))),
        check_vma=False,
    )
```

```python
import functools

import jax
import jax.numpy as jnp
from jax import lax
from jax.experimental import pallas as pl
from jax.experimental.pallas import tpu as pltpu
from jax.sharding import PartitionSpec as P

STEPS = 4
SLOTS = 32
HALO = 2 * STEPS
LANES = 128
F32 = jnp.float32
BF16 = jnp.bfloat16
I32 = jnp.int32

WHOLE = pl.BlockSpec(memory_space=pltpu.VMEM)
AWAY = pl.BlockSpec(memory_space=pl.ANY)


def call(kernel, outs, scratch=(), limit=24 << 20, place=WHOLE):
    def run(*operands):
        return pl.pallas_call(
            kernel,
            out_shape=outs,
            in_specs=[place] * len(operands),
            out_specs=jax.tree.map(lambda _: WHOLE, outs),
            scratch_shapes=list(scratch),
            compiler_params=pltpu.CompilerParams(vmem_limit_bytes=limit),
        )(*operands)

    return run


def halves(value):
    high = value.astype(BF16).astype(F32)
    return high, value - high


def nt_dot(a, b):
    return lax.dot_general(a, b, (((1,), (1,)), ((), ())), preferred_element_type=F32)


def bring(away_refs, near_refs, sem_ref):
    copies = [
        pltpu.make_async_copy(away, near, sem_ref.at[i])
        for i, (away, near) in enumerate(zip(away_refs, near_refs))
    ]
    for copy in copies:
        copy.start()
    for copy in copies:
        copy.wait()


def pack_kernel(*refs):
    out_ref, rank_ref = refs[4:6]
    owner_ref, cell_ref, depart_ref, weight_ref = refs[6:10]
    bring(refs[:4], refs[6:10], refs[10])
    places = out_ref.shape[0]
    chunks = owner_ref.shape[0]
    dest_ids = lax.broadcasted_iota(I32, (places, LANES), 0)
    slot_ids = lax.broadcasted_iota(I32, (SLOTS, LANES), 0).astype(F32)
    source = lax.broadcasted_iota(I32, (LANES, 2 * LANES), 0)
    target = lax.broadcasted_iota(I32, (LANES, 2 * LANES), 1)
    counter = jnp.where(source <= target, 1.0, 0.0).astype(BF16)
    seen = jnp.full((places, LANES), -1.0, F32)
    packed = jnp.zeros((places, 6 * SLOTS), F32)
    for j in range(chunks):
        hit = dest_ids == owner_ref[j : j + 1, :]
        names = jnp.where(hit, 1.0, 0.0).astype(BF16)
        counts = jnp.dot(names, counter, preferred_element_type=F32)
        rank = jnp.sum(jnp.where(hit, counts[:, :LANES] + seen, 0.0), axis=0, keepdims=True)
        seen = seen + counts[:, LANES:]
        rank_ref[j : j + 1, :] = rank
        weight = weight_ref[j : j + 1, :]
        product_high, product_low = halves(weight * depart_ref[j : j + 1, :])
        weight_high, weight_low = halves(weight)
        cell = cell_ref[j : j + 1, :]
        row = (cell // 256).astype(F32)
        col = (cell % 256).astype(F32)
        chosen = slot_ids == rank
        fields = [
            jnp.where(chosen, field, 0.0)
            for field in (product_high, weight_high, row, col, product_low, weight_low)
        ]
        packed = packed + nt_dot(names, jnp.concatenate(fields, axis=0).astype(BF16))
    low = jnp.concatenate(
        [packed[:, 4 * SLOTS :], jnp.zeros((places, 2 * SLOTS), F32)], axis=1
    )
    out_ref[...] = packed[:, : 4 * SLOTS] + low


def scatter_kernel(got_ref, out_ref, turned_ref):
    rows, cols = 64, 256
    turned_ref[...] = got_ref[...].T
    width = turned_ref.shape[1]
    row_ids = lax.broadcasted_iota(I32, (rows, width), 0).astype(F32)
    col_ids = lax.broadcasted_iota(I32, (cols, width), 0).astype(F32)
    total = jnp.zeros((4 * rows, cols), F32)
    for s in range(0, SLOTS, 2):
        left, right = [], []
        for k in (s, s + 1):
            product_high, product_low = halves(turned_ref[k : k + 1, :])
            weight_high, weight_low = halves(turned_ref[SLOTS + k : SLOTS + k + 1, :])
            in_row = row_ids == turned_ref[2 * SLOTS + k : 2 * SLOTS + k + 1, :]
            in_col = col_ids == turned_ref[3 * SLOTS + k : 3 * SLOTS + k + 1, :]
            left.append(
                jnp.concatenate(
                    [
                        jnp.where(in_row, v, 0.0)
                        for v in (product_high, product_low, weight_high, weight_low)
                    ],
                    axis=0,
                ).astype(BF16)
            )
            right.append(jnp.where(in_col, 1.0, 0.0).astype(BF16))
        total = total + nt_dot(jnp.concatenate(left, axis=1), jnp.concatenate(right, axis=1))
    product = total[:rows] + total[rows : 2 * rows]
    weight = total[2 * rows : 3 * rows] + total[3 * rows :]
    quarters, width = out_ref.shape[0], out_ref.shape[2] // 2
    for q in range(quarters):
        out_ref[q, :, :width] = product[:, q * width : (q + 1) * width]
        out_ref[q, :, width:] = weight[:, q * width : (q + 1) * width]


def quarter_kernel(members_ref, own_ref, *rest):
    sent_refs, kept_ref = rest[:-1], rest[-1]
    members = members_ref.shape[0]
    quarters = kept_ref.shape[0]
    width = members_ref.shape[2] // quarters
    for k in range(members):
        value = members_ref[k].astype(F32)
        for q in range(quarters):
            kept_ref[q, :, k * width : (k + 1) * width] = value[:, q * width : (q + 1) * width]
    mine = lax.axis_index("mem")
    own_ref[...] = kept_ref[mine]
    for k, ref in enumerate(sent_refs):
        ref[...] = kept_ref[(mine + k + 1) % quarters]


def reduce_kernel(parts_ref, rate_ref, sea_ref, *rest):
    quarters = parts_ref.shape[0]
    piece_refs, (mid_ref, one_ref, two_ref, kept_ref) = rest[:quarters], rest[quarters:]
    rows, lanes = piece_refs[0].shape
    width = parts_ref.shape[2] // 2
    mine = lax.axis_index("mem")
    for k in range(quarters):
        mid_ref[(mine - k + quarters) % quarters, :, :lanes] = piece_refs[k][...]
    whole = parts_ref[0]
    for q in range(1, quarters):
        whole = whole + parts_ref[q]
    mid_ref[0, :, lanes:] = whole
    for q in range(quarters):
        at = slice(q * width, (q + 1) * width)
        kept_ref[q, :, :width] = rate_ref[:, at]
        kept_ref[q, :, width:] = sea_ref[:, at].astype(F32)
    mid_ref[1, :, lanes:] = kept_ref[mine]
    even = lax.axis_index("lat") % 2 == 0
    for q in range(quarters):
        size = lanes if q > 1 else lanes + 2 * width
        top, bottom = mid_ref[q, :HALO, :size], mid_ref[q, rows - HALO :, :size]
        one_ref[q, :, :size] = jnp.where(even, bottom, top)
        two_ref[q, :, :size] = jnp.where(even, top, bottom)
        if size < one_ref.shape[2]:
            one_ref[q, :, size:] = jnp.zeros((HALO, 2 * width), F32)
            two_ref[q, :, size:] = jnp.zeros((HALO, 2 * width), F32)


def fields_of(ref, width):
    quarters, lanes = ref.shape[0], ref.shape[2] - 2 * width
    places = [(q, k * width) for q in range(quarters) for k in range(lanes // width)]
    return places + [(0, lanes), (0, lanes + width), (1, lanes), (1, lanes + width)]


def rim_kernel(
    mid_ref, got_one_ref, got_two_ref, one_ref, two_ref, north_ref, south_ref, first_ref, last_ref, *, width
):
    rows, lanes = mid_ref.shape[1], mid_ref.shape[2]
    lat = lax.axis_index("lat")
    even = lat % 2 == 0
    north_ref[...] = jnp.where(even, got_two_ref[...], got_one_ref[...])
    south_ref[...] = jnp.where(even, got_one_ref[...], got_two_ref[...])
    sea = slice(lanes - width, lanes)
    north_ref[1, :, sea] = jnp.where(lat == 0, 0.0, north_ref[1, :, sea])
    south_ref[1, :, sea] = jnp.where(lat == lax.axis_size("lat") - 1, 0.0, south_ref[1, :, sea])
    first_ref[...] = jnp.zeros(first_ref.shape, F32)
    last_ref[...] = jnp.zeros(last_ref.shape, F32)
    for k, (q, lane) in enumerate(fields_of(mid_ref, width)):
        at = slice(k * HALO, (k + 1) * HALO)
        for ref, cut in ((first_ref, lane), (last_ref, lane + width - HALO)):
            ref[:HALO, at] = north_ref[q, :, cut : cut + HALO]
            ref[HALO : HALO + rows, at] = mid_ref[q, :, cut : cut + HALO]
            ref[HALO + rows :, at] = south_ref[q, :, cut : cut + HALO]
    even = lax.axis_index("mem") % 2 == 0
    one_ref[...] = jnp.where(even, last_ref[...], first_ref[...])
    two_ref[...] = jnp.where(even, first_ref[...], last_ref[...])


def product_kernel(
    mid_ref, north_ref, south_ref, one_ref, two_ref, out_ref,
    members_ref, state_ref, weights_ref, tiled_ref, field_ref, west_ref, east_ref,
):
    groups, height, lanes = members_ref.shape
    rows = height - 2 * HALO
    width = out_ref.shape[2] // 2
    span = width + 2 * HALO
    windows = lanes // span
    divisor = groups * windows - 1
    pad = 8

    def tile_lanes(value):
        for k in range(windows):
            tiled_ref[:, k * span : (k + 1) * span] = value
        return tiled_ref[...]

    even = lax.axis_index("mem") % 2 == 0
    west_ref[...] = jnp.where(even, two_ref[...], one_ref[...])
    east_ref[...] = jnp.where(even, one_ref[...], two_ref[...])
    for k, (q, lane) in enumerate(fields_of(mid_ref, width)):
        rim = slice(k * HALO, (k + 1) * HALO)
        cut = slice(lane, lane + width)
        north, south = north_ref[q, :, cut], south_ref[q, :, cut]
        if k < groups * windows:
            ref, low = members_ref.at[k // windows], k % windows * span
        else:
            ref, low = field_ref.at[k - groups * windows], 0
        ref[:, low : low + HALO] = west_ref[:, rim]
        ref[:HALO, low + HALO : low + HALO + width] = north
        ref[HALO : HALO + rows, low + HALO : low + HALO + width] = mid_ref[q, :, cut]
        ref[HALO + rows :, low + HALO : low + HALO + width] = south
        ref[:, low + HALO + width : low + span] = east_ref[:, rim]
    innovation = field_ref[0, :, :span]
    weight_sum = field_ref[1, :, :span]
    sea_cover = field_ref[3, :, :span]

    rate = tile_lanes(field_ref[2, :, :span])
    sea = tile_lanes(sea_cover)
    north = 0.5 * (rate + pltpu.roll(rate, height - 1, 0)) * sea * pltpu.roll(sea, height - 1, 0)
    east = 0.5 * (rate + pltpu.roll(rate, lanes - 1, 1)) * sea * pltpu.roll(sea, lanes - 1, 1)
    south = pltpu.roll(north, 1, 0)
    west = pltpu.roll(east, 1, 1)
    weights_ref[0] = 1.0 - (north + south + east + west)
    weights_ref[1] = north
    weights_ref[2] = south
    weights_ref[3] = east
    weights_ref[4] = west
    state_ref[...] = jnp.zeros(state_ref.shape, F32)

    def sweep(source, target):
        for r in range(0, height, 8):
            centre_w, north_w, south_w, east_w, west_w = (
                weights_ref[i, r : r + 8, :] for i in range(5)
            )
            for g in range(groups):
                centre = state_ref[source, g, pad + r : pad + r + 8, :]
                above = state_ref[source, g, pad + r + 1 : pad + r + 9, :]
                below = state_ref[source, g, pad + r - 1 : pad + r + 7, :]
                state_ref[target, g, pad + r : pad + r + 8, :] = (
                    centre_w * centre
                    + (north_w * above + south_w * below)
                    + (east_w * pltpu.roll(centre, lanes - 1, 1) + west_w * pltpu.roll(centre, 1, 1))
                )

    def covariance(source):
        tiled = tile_lanes(source)
        for g in range(groups):
            state_ref[0, g, pad : pad + height, :] = members_ref[g] * tiled

        def pair(_, carry):
            sweep(0, 1)
            sweep(1, 0)
            return carry

        lax.fori_loop(0, STEPS // 2, pair, 0)
        total = members_ref[0] * state_ref[0, 0, pad : pad + height, :]
        for g in range(1, groups):
            total = total + members_ref[g] * state_ref[0, g, pad : pad + height, :]
        tiled_ref[...] = total
        summed = tiled_ref[:, :span]
        for k in range(1, windows):
            summed = summed + tiled_ref[:, k * span : (k + 1) * span]
        return sea_cover * summed / divisor

    first_pass = covariance(innovation)
    increment = covariance(innovation - weight_sum * first_pass)
    field_ref[0, :, :span] = increment
    half = (height - 2 * HALO) // 2
    for q in range(out_ref.shape[0]):
        out_ref[q, :, :width] = field_ref[0, HALO : HALO + half, HALO : HALO + width]
        out_ref[q, :, width:] = field_ref[0, HALO + half : HALO + 2 * half, HALO : HALO + width]


def answer_kernel(pieces_ref, turned_ref, tile_ref, out_ref, reply_ref):
    quarters, half, width = pieces_ref.shape[0], pieces_ref.shape[1], pieces_ref.shape[2] // 2
    rows, cols = tile_ref.shape
    for q in range(quarters):
        tile_ref[:half, q * width : (q + 1) * width] = pieces_ref[q, :, :width]
        tile_ref[half:, q * width : (q + 1) * width] = pieces_ref[q, :, width:]
    high, low = halves(tile_ref[...])
    both = jnp.concatenate([high, low], axis=0).astype(BF16)
    lanes = turned_ref.shape[1]
    row_ids = lax.broadcasted_iota(I32, (rows, lanes), 0).astype(F32)
    col_ids = lax.broadcasted_iota(I32, (cols, lanes), 0).astype(F32)
    reply_ref[...] = jnp.zeros(reply_ref.shape, F32)
    for k in range(SLOTS):
        in_row = row_ids == turned_ref[2 * SLOTS + k : 2 * SLOTS + k + 1, :]
        in_col = col_ids == turned_ref[3 * SLOTS + k : 3 * SLOTS + k + 1, :]
        picked = jnp.dot(both, jnp.where(in_col, 1.0, 0.0).astype(BF16), preferred_element_type=F32)
        picked = picked[:rows] + picked[rows:]
        reply_ref[k : k + 1, :] = jnp.sum(jnp.where(in_row, picked, 0.0), axis=0, keepdims=True)
    out_ref[...] = reply_ref[...].T[:, :SLOTS]


def residual_kernel(owner_ref, rank_ref, depart_ref, got_ref, out_ref, wide_ref):
    places = got_ref.shape[0]
    chunks = owner_ref.shape[0]
    wide_ref[...] = jnp.zeros(wide_ref.shape, F32)
    wide_ref[:places, :SLOTS] = got_ref[...]
    turned = wide_ref[...].T[:SLOTS, :]
    high, low = halves(turned)
    both = jnp.concatenate([high, low], axis=0).astype(BF16)
    dest_ids = lax.broadcasted_iota(I32, (wide_ref.shape[0], LANES), 0)
    slot_ids = lax.broadcasted_iota(I32, (SLOTS, LANES), 0).astype(F32)
    for j in range(chunks):
        names = jnp.where(dest_ids == owner_ref[j : j + 1, :], 1.0, 0.0).astype(BF16)
        picked = jnp.dot(both, names, preferred_element_type=F32)
        picked = picked[:SLOTS] + picked[SLOTS:]
        value = jnp.sum(
            jnp.where(slot_ids == rank_ref[j : j + 1, :], picked, 0.0), axis=0, keepdims=True
        )
        out_ref[j : j + 1, :] = depart_ref[j : j + 1, :] - value


def shape(*dims, dtype=F32):
    return jax.ShapeDtypeStruct(dims, dtype)


def exchange(first, second, axes):
    size = 1
    for axis in axes:
        size *= lax.axis_size(axis)
    swaps = [[(i + k, (i + k + 1) % size) for i in range(0, size, 2)] for k in range(2)]
    both = [pairs + [(j, i) for i, j in pairs] for pairs in swaps]
    return lax.ppermute(first, axes, both[0]), lax.ppermute(second, axes, both[1])


def per_device(perturbations, diffusivity, sea_mask, obs_owner, obs_cell, obs_depart, obs_weight):
    members, rows, cols = perturbations.shape
    quarters = lax.axis_size("mem")
    places = lax.axis_size("lat") * lax.axis_size("lon")
    width = cols // quarters
    span = width + 2 * HALO
    height = rows + 2 * HALO
    chunks = obs_cell.shape[0] // LANES
    owner, cell, depart, weight = (
        a.reshape(chunks, LANES) for a in (obs_owner, obs_cell, obs_depart, obs_weight)
    )
    tiles = ("lat", "lon")

    piece = shape(rows, members * width)
    own, *sent = call(quarter_kernel, [piece] * quarters, [pltpu.VMEM((quarters, rows, members * width), F32)])(
        perturbations
    )
    ring = [
        [(i, (i + k) % quarters) for i in range(quarters)] for k in range(1, quarters)
    ]
    outgoing, rank = call(
        pack_kernel,
        (shape(places, LANES), shape(chunks, LANES)),
        [pltpu.VMEM((chunks, LANES), a.dtype) for a in (owner, cell, depart, weight)]
        + [pltpu.SemaphoreType.DMA((4,))],
        place=AWAY,
    )(owner, cell, depart, weight)
    got = lax.all_to_all(outgoing, tiles, split_axis=0, concat_axis=0, tiled=True)
    brought = [lax.ppermute(s, "mem", pairs) for s, pairs in zip(sent, ring)]
    got, *brought = lax.optimization_barrier((got, *brought))

    parts, turned = call(
        scatter_kernel, (shape(quarters, rows, 2 * width), shape(LANES, places))
    )(got)
    parts = lax.all_to_all(parts, "mem", split_axis=0, concat_axis=0, tiled=True)
    field_lanes = members * width + 2 * width
    strip = shape(quarters, HALO, field_lanes)
    mid, one, two = call(
        reduce_kernel,
        (shape(quarters, rows, field_lanes), strip, strip),
        [pltpu.VMEM((quarters, rows, 2 * width), F32)],
    )(parts, diffusivity, sea_mask, own, *brought)
    one, two = exchange(one, two, ("lat",))
    rim_lanes = -(-(quarters * members + 4) * HALO // LANES) * LANES
    rim = shape(height, rim_lanes)
    one, two, north, south = call(
        functools.partial(rim_kernel, width=width),
        (rim, rim, strip, strip),
        [pltpu.VMEM((height, rim_lanes), F32)] * 2,
    )(mid, one, two)
    one, two = exchange(one, two, ("lon", "mem"))
    lanes = members * span
    quarter = call(
        product_kernel,
        shape(quarters, rows // 2, 2 * width),
        [
            pltpu.VMEM((quarters, height, lanes), F32),
            pltpu.VMEM((2, quarters, height + 16, lanes), F32),
            pltpu.VMEM((5, height, lanes), F32),
            pltpu.VMEM((height, lanes), F32),
            pltpu.VMEM((4, height, LANES), F32),
            pltpu.VMEM((height, rim_lanes), F32),
            pltpu.VMEM((height, rim_lanes), F32),
        ],
    )(mid, north, south, one, two)
    quarter = lax.all_to_all(quarter, "mem", split_axis=0, concat_axis=0, tiled=True)
    increment, answers = call(
        answer_kernel, (shape(rows, cols), shape(places, SLOTS)), [pltpu.VMEM((LANES, places), F32)]
    )(quarter, turned)
    returned = lax.all_to_all(answers, tiles, split_axis=0, concat_axis=0, tiled=True)
    residual = call(
        residual_kernel, shape(chunks, LANES), [pltpu.VMEM((max(LANES, places), LANES), F32)]
    )(owner, rank, depart, returned)
    return increment, residual.reshape(chunks * LANES)


def solution(mesh):
    return jax.shard_map(
        per_device,
        mesh=mesh,
        in_specs=(
            P("mem", "lat", "lon"),
            P("lat", "lon"),
            P("lat", "lon"),
            P(("lat", "lon", "mem"), None),
            P(("lat", "lon", "mem")),
            P(("lat", "lon", "mem")),
            P(("lat", "lon", "mem")),
        ),
        out_specs=(P("lat", "lon"), P(("lat", "lon", "mem"))),
        check_vma=False,
    )
```

```python
import functools

import jax
import jax.numpy as jnp
from jax import lax
from jax.experimental import pallas as pl
from jax.experimental.pallas import tpu as pltpu
from jax.sharding import PartitionSpec as P

STEPS = 4
SLOTS = 32
HALO = 2 * STEPS
LANES = 128
F32 = jnp.float32
BF16 = jnp.bfloat16
I32 = jnp.int32

WHOLE = pl.BlockSpec(memory_space=pltpu.VMEM)
AWAY = pl.BlockSpec(memory_space=pl.ANY)


def call(kernel, outs, scratch=(), limit=24 << 20, place=WHOLE):
    def run(*operands):
        return pl.pallas_call(
            kernel,
            out_shape=outs,
            in_specs=[place] * len(operands),
            out_specs=jax.tree.map(lambda _: WHOLE, outs),
            scratch_shapes=list(scratch),
            compiler_params=pltpu.CompilerParams(vmem_limit_bytes=limit),
        )(*operands)

    return run


def halves(value):
    high = value.astype(BF16).astype(F32)
    return high, value - high


def nt_dot(a, b):
    return lax.dot_general(a, b, (((1,), (1,)), ((), ())), preferred_element_type=F32)


def bring(away_refs, near_refs, sem_ref):
    copies = [
        pltpu.make_async_copy(away, near, sem_ref.at[i])
        for i, (away, near) in enumerate(zip(away_refs, near_refs))
    ]
    for copy in copies:
        copy.start()
    for copy in copies:
        copy.wait()


def pack_kernel(*refs):
    out_ref, rank_ref = refs[4:6]
    owner_ref, cell_ref, depart_ref, weight_ref = refs[6:10]
    bring(refs[:4], refs[6:10], refs[10])
    places = out_ref.shape[0]
    chunks = owner_ref.shape[0]
    dest_ids = lax.broadcasted_iota(I32, (places, LANES), 0)
    slot_ids = lax.broadcasted_iota(I32, (SLOTS, LANES), 0).astype(F32)
    source = lax.broadcasted_iota(I32, (LANES, 2 * LANES), 0)
    target = lax.broadcasted_iota(I32, (LANES, 2 * LANES), 1)
    counter = jnp.where(source <= target, 1.0, 0.0).astype(BF16)
    seen = jnp.full((places, LANES), -1.0, F32)
    packed = jnp.zeros((places, 6 * SLOTS), F32)
    for j in range(chunks):
        hit = dest_ids == owner_ref[j : j + 1, :]
        names = jnp.where(hit, 1.0, 0.0).astype(BF16)
        counts = jnp.dot(names, counter, preferred_element_type=F32)
        rank = jnp.sum(jnp.where(hit, counts[:, :LANES] + seen, 0.0), axis=0, keepdims=True)
        seen = seen + counts[:, LANES:]
        rank_ref[j : j + 1, :] = rank
        weight = weight_ref[j : j + 1, :]
        product_high, product_low = halves(weight * depart_ref[j : j + 1, :])
        weight_high, weight_low = halves(weight)
        cell = cell_ref[j : j + 1, :]
        row = (cell // 256).astype(F32)
        col = (cell % 256).astype(F32)
        chosen = slot_ids == rank
        fields = [
            jnp.where(chosen, field, 0.0)
            for field in (product_high, weight_high, row, col, product_low, weight_low)
        ]
        packed = packed + nt_dot(names, jnp.concatenate(fields, axis=0).astype(BF16))
    low = jnp.concatenate(
        [packed[:, 4 * SLOTS :], jnp.zeros((places, 2 * SLOTS), F32)], axis=1
    )
    out_ref[...] = packed[:, : 4 * SLOTS] + low


def scatter_kernel(got_ref, out_ref, turned_ref):
    rows, cols = 64, 256
    turned_ref[...] = got_ref[...].T
    width = turned_ref.shape[1]
    row_ids = lax.broadcasted_iota(I32, (rows, width), 0).astype(F32)
    col_ids = lax.broadcasted_iota(I32, (cols, width), 0).astype(F32)
    total = jnp.zeros((4 * rows, cols), F32)
    for s in range(0, SLOTS, 2):
        left, right = [], []
        for k in (s, s + 1):
            product_high, product_low = halves(turned_ref[k : k + 1, :])
            weight_high, weight_low = halves(turned_ref[SLOTS + k : SLOTS + k + 1, :])
            in_row = row_ids == turned_ref[2 * SLOTS + k : 2 * SLOTS + k + 1, :]
            in_col = col_ids == turned_ref[3 * SLOTS + k : 3 * SLOTS + k + 1, :]
            left.append(
                jnp.concatenate(
                    [
                        jnp.where(in_row, v, 0.0)
                        for v in (product_high, product_low, weight_high, weight_low)
                    ],
                    axis=0,
                ).astype(BF16)
            )
            right.append(jnp.where(in_col, 1.0, 0.0).astype(BF16))
        total = total + nt_dot(jnp.concatenate(left, axis=1), jnp.concatenate(right, axis=1))
    product = total[:rows] + total[rows : 2 * rows]
    weight = total[2 * rows : 3 * rows] + total[3 * rows :]
    quarters, width = out_ref.shape[0], out_ref.shape[2] // 2
    for q in range(quarters):
        out_ref[q, :, :width] = product[:, q * width : (q + 1) * width]
        out_ref[q, :, width:] = weight[:, q * width : (q + 1) * width]


def quarter_kernel(members_ref, own_ref, *rest):
    sent_refs, kept_ref = rest[:-1], rest[-1]
    members = members_ref.shape[0]
    quarters = kept_ref.shape[0]
    width = members_ref.shape[2] // quarters
    for k in range(members):
        value = members_ref[k].astype(F32)
        for q in range(quarters):
            kept_ref[q, :, k * width : (k + 1) * width] = value[:, q * width : (q + 1) * width]
    mine = lax.axis_index("mem")
    own_ref[...] = kept_ref[mine]
    for k, ref in enumerate(sent_refs):
        ref[...] = kept_ref[(mine + k + 1) % quarters]


def reduce_kernel(parts_ref, rate_ref, sea_ref, *rest):
    quarters = parts_ref.shape[0]
    piece_refs, (mid_ref, top_ref, bottom_ref, kept_ref) = rest[:quarters], rest[quarters:]
    rows, lanes = piece_refs[0].shape
    width = parts_ref.shape[2] // 2
    mine = lax.axis_index("mem")
    for k in range(quarters):
        mid_ref[(mine - k + quarters) % quarters, :, :lanes] = piece_refs[k][...]
    whole = parts_ref[0]
    for q in range(1, quarters):
        whole = whole + parts_ref[q]
    mid_ref[0, :, lanes:] = whole
    for q in range(quarters):
        at = slice(q * width, (q + 1) * width)
        kept_ref[q, :, :width] = rate_ref[:, at]
        kept_ref[q, :, width:] = sea_ref[:, at].astype(F32)
    mid_ref[1, :, lanes:] = kept_ref[mine]
    for q in range(quarters):
        size = lanes if q > 1 else lanes + 2 * width
        top_ref[q, :, :size] = mid_ref[q, :HALO, :size]
        bottom_ref[q, :, :size] = mid_ref[q, rows - HALO :, :size]
        if size < top_ref.shape[2]:
            top_ref[q, :, size:] = jnp.zeros((HALO, 2 * width), F32)
            bottom_ref[q, :, size:] = jnp.zeros((HALO, 2 * width), F32)


def fields_of(ref, width):
    quarters, lanes = ref.shape[0], ref.shape[2] - 2 * width
    places = [(q, k * width) for q in range(quarters) for k in range(lanes // width)]
    return places + [(0, lanes), (0, lanes + width), (1, lanes), (1, lanes + width)]


def rim_kernel(
    mid_ref, before_ref, after_ref, one_ref, two_ref, north_ref, south_ref, first_ref, last_ref, *, width
):
    rows, lanes = mid_ref.shape[1], mid_ref.shape[2]
    lat = lax.axis_index("lat")
    north_ref[...] = before_ref[...]
    south_ref[...] = after_ref[...]
    sea = slice(lanes - width, lanes)
    north_ref[1, :, sea] = jnp.where(lat == 0, 0.0, north_ref[1, :, sea])
    south_ref[1, :, sea] = jnp.where(lat == lax.axis_size("lat") - 1, 0.0, south_ref[1, :, sea])
    first_ref[...] = jnp.zeros(first_ref.shape, F32)
    last_ref[...] = jnp.zeros(last_ref.shape, F32)
    for k, (q, lane) in enumerate(fields_of(mid_ref, width)):
        at = slice(k * HALO, (k + 1) * HALO)
        for ref, cut in ((first_ref, lane), (last_ref, lane + width - HALO)):
            ref[:HALO, at] = north_ref[q, :, cut : cut + HALO]
            ref[HALO : HALO + rows, at] = mid_ref[q, :, cut : cut + HALO]
            ref[HALO + rows :, at] = south_ref[q, :, cut : cut + HALO]
    even = lax.axis_index("mem") % 2 == 0
    one_ref[...] = jnp.where(even, last_ref[...], first_ref[...])
    two_ref[...] = jnp.where(even, first_ref[...], last_ref[...])


def product_kernel(
    mid_ref, north_ref, south_ref, one_ref, two_ref, out_ref,
    members_ref, state_ref, weights_ref, tiled_ref, field_ref, west_ref, east_ref,
):
    groups, height, lanes = members_ref.shape
    rows = height - 2 * HALO
    width = out_ref.shape[2] // 2
    span = width + 2 * HALO
    windows = lanes // span
    divisor = groups * windows - 1
    pad = 8

    def tile_lanes(value):
        for k in range(windows):
            tiled_ref[:, k * span : (k + 1) * span] = value
        return tiled_ref[...]

    even = lax.axis_index("mem") % 2 == 0
    west_ref[...] = jnp.where(even, two_ref[...], one_ref[...])
    east_ref[...] = jnp.where(even, one_ref[...], two_ref[...])
    for k, (q, lane) in enumerate(fields_of(mid_ref, width)):
        rim = slice(k * HALO, (k + 1) * HALO)
        cut = slice(lane, lane + width)
        north, south = north_ref[q, :, cut], south_ref[q, :, cut]
        if k < groups * windows:
            ref, low = members_ref.at[k // windows], k % windows * span
        else:
            ref, low = field_ref.at[k - groups * windows], 0
        ref[:, low : low + HALO] = west_ref[:, rim]
        ref[:HALO, low + HALO : low + HALO + width] = north
        ref[HALO : HALO + rows, low + HALO : low + HALO + width] = mid_ref[q, :, cut]
        ref[HALO + rows :, low + HALO : low + HALO + width] = south
        ref[:, low + HALO + width : low + span] = east_ref[:, rim]
    innovation = field_ref[0, :, :span]
    weight_sum = field_ref[1, :, :span]
    sea_cover = field_ref[3, :, :span]

    rate = tile_lanes(field_ref[2, :, :span])
    sea = tile_lanes(sea_cover)
    north = 0.5 * (rate + pltpu.roll(rate, height - 1, 0)) * sea * pltpu.roll(sea, height - 1, 0)
    east = 0.5 * (rate + pltpu.roll(rate, lanes - 1, 1)) * sea * pltpu.roll(sea, lanes - 1, 1)
    south = pltpu.roll(north, 1, 0)
    west = pltpu.roll(east, 1, 1)
    weights_ref[0] = 1.0 - (north + south + east + west)
    weights_ref[1] = north
    weights_ref[2] = south
    weights_ref[3] = east
    weights_ref[4] = west
    state_ref[...] = jnp.zeros(state_ref.shape, F32)

    def sweep(source, target):
        for r in range(0, height, 8):
            centre_w, north_w, south_w, east_w, west_w = (
                weights_ref[i, r : r + 8, :] for i in range(5)
            )
            for g in range(groups):
                centre = state_ref[source, g, pad + r : pad + r + 8, :]
                above = state_ref[source, g, pad + r + 1 : pad + r + 9, :]
                below = state_ref[source, g, pad + r - 1 : pad + r + 7, :]
                state_ref[target, g, pad + r : pad + r + 8, :] = (
                    centre_w * centre
                    + (north_w * above + south_w * below)
                    + (east_w * pltpu.roll(centre, lanes - 1, 1) + west_w * pltpu.roll(centre, 1, 1))
                )

    def covariance(source):
        tiled = tile_lanes(source)
        for g in range(groups):
            state_ref[0, g, pad : pad + height, :] = members_ref[g] * tiled

        def pair(_, carry):
            sweep(0, 1)
            sweep(1, 0)
            return carry

        lax.fori_loop(0, STEPS // 2, pair, 0)
        total = members_ref[0] * state_ref[0, 0, pad : pad + height, :]
        for g in range(1, groups):
            total = total + members_ref[g] * state_ref[0, g, pad : pad + height, :]
        tiled_ref[...] = total
        summed = tiled_ref[:, :span]
        for k in range(1, windows):
            summed = summed + tiled_ref[:, k * span : (k + 1) * span]
        return sea_cover * summed / divisor

    first_pass = covariance(innovation)
    increment = covariance(innovation - weight_sum * first_pass)
    field_ref[0, :, :span] = increment
    half = (height - 2 * HALO) // 2
    for q in range(out_ref.shape[0]):
        out_ref[q, :, :width] = field_ref[0, HALO : HALO + half, HALO : HALO + width]
        out_ref[q, :, width:] = field_ref[0, HALO + half : HALO + 2 * half, HALO : HALO + width]


def answer_kernel(pieces_ref, turned_ref, tile_ref, out_ref, reply_ref):
    quarters, half, width = pieces_ref.shape[0], pieces_ref.shape[1], pieces_ref.shape[2] // 2
    rows, cols = tile_ref.shape
    for q in range(quarters):
        tile_ref[:half, q * width : (q + 1) * width] = pieces_ref[q, :, :width]
        tile_ref[half:, q * width : (q + 1) * width] = pieces_ref[q, :, width:]
    high, low = halves(tile_ref[...])
    both = jnp.concatenate([high, low], axis=0).astype(BF16)
    lanes = turned_ref.shape[1]
    row_ids = lax.broadcasted_iota(I32, (rows, lanes), 0).astype(F32)
    col_ids = lax.broadcasted_iota(I32, (cols, lanes), 0).astype(F32)
    reply_ref[...] = jnp.zeros(reply_ref.shape, F32)
    for k in range(SLOTS):
        in_row = row_ids == turned_ref[2 * SLOTS + k : 2 * SLOTS + k + 1, :]
        in_col = col_ids == turned_ref[3 * SLOTS + k : 3 * SLOTS + k + 1, :]
        picked = jnp.dot(both, jnp.where(in_col, 1.0, 0.0).astype(BF16), preferred_element_type=F32)
        picked = picked[:rows] + picked[rows:]
        reply_ref[k : k + 1, :] = jnp.sum(jnp.where(in_row, picked, 0.0), axis=0, keepdims=True)
    out_ref[...] = reply_ref[...].T[:, :SLOTS]


def residual_kernel(owner_ref, rank_ref, depart_ref, got_ref, out_ref, wide_ref):
    places = got_ref.shape[0]
    chunks = owner_ref.shape[0]
    wide_ref[...] = jnp.zeros(wide_ref.shape, F32)
    wide_ref[:places, :SLOTS] = got_ref[...]
    turned = wide_ref[...].T[:SLOTS, :]
    high, low = halves(turned)
    both = jnp.concatenate([high, low], axis=0).astype(BF16)
    dest_ids = lax.broadcasted_iota(I32, (wide_ref.shape[0], LANES), 0)
    slot_ids = lax.broadcasted_iota(I32, (SLOTS, LANES), 0).astype(F32)
    for j in range(chunks):
        names = jnp.where(dest_ids == owner_ref[j : j + 1, :], 1.0, 0.0).astype(BF16)
        picked = jnp.dot(both, names, preferred_element_type=F32)
        picked = picked[:SLOTS] + picked[SLOTS:]
        value = jnp.sum(
            jnp.where(slot_ids == rank_ref[j : j + 1, :], picked, 0.0), axis=0, keepdims=True
        )
        out_ref[j : j + 1, :] = depart_ref[j : j + 1, :] - value


def shape(*dims, dtype=F32):
    return jax.ShapeDtypeStruct(dims, dtype)


def shift(first, last, axis):
    size = lax.axis_size(axis)
    up = [(i, (i + 1) % size) for i in range(size)]
    return lax.ppermute(last, axis, up), lax.ppermute(first, axis, [(j, i) for i, j in up])


def exchange(first, second, axes):
    size = 1
    for axis in axes:
        size *= lax.axis_size(axis)
    swaps = [[(i + k, (i + k + 1) % size) for i in range(0, size, 2)] for k in range(2)]
    both = [pairs + [(j, i) for i, j in pairs] for pairs in swaps]
    return lax.ppermute(first, axes, both[0]), lax.ppermute(second, axes, both[1])


def per_device(perturbations, diffusivity, sea_mask, obs_owner, obs_cell, obs_depart, obs_weight):
    members, rows, cols = perturbations.shape
    quarters = lax.axis_size("mem")
    places = lax.axis_size("lat") * lax.axis_size("lon")
    width = cols // quarters
    span = width + 2 * HALO
    height = rows + 2 * HALO
    chunks = obs_cell.shape[0] // LANES
    owner, cell, depart, weight = (
        a.reshape(chunks, LANES) for a in (obs_owner, obs_cell, obs_depart, obs_weight)
    )
    tiles = ("lat", "lon")

    piece = shape(rows, members * width)
    own, *sent = call(quarter_kernel, [piece] * quarters, [pltpu.VMEM((quarters, rows, members * width), F32)])(
        perturbations
    )
    ring = [
        [(i, (i + k) % quarters) for i in range(quarters)] for k in range(1, quarters)
    ]
    outgoing, rank = call(
        pack_kernel,
        (shape(places, LANES), shape(chunks, LANES)),
        [pltpu.VMEM((chunks, LANES), a.dtype) for a in (owner, cell, depart, weight)]
        + [pltpu.SemaphoreType.DMA((4,))],
        place=AWAY,
    )(owner, cell, depart, weight)
    got = lax.all_to_all(outgoing, tiles, split_axis=0, concat_axis=0, tiled=True)
    brought = [lax.ppermute(s, "mem", pairs) for s, pairs in zip(sent, ring)]
    got, *brought = lax.optimization_barrier((got, *brought))

    parts, turned = call(
        scatter_kernel, (shape(quarters, rows, 2 * width), shape(LANES, places))
    )(got)
    parts = lax.all_to_all(parts, "mem", split_axis=0, concat_axis=0, tiled=True)
    field_lanes = members * width + 2 * width
    strip = shape(quarters, HALO, field_lanes)
    mid, top, bottom = call(
        reduce_kernel,
        (shape(quarters, rows, field_lanes), strip, strip),
        [pltpu.VMEM((quarters, rows, 2 * width), F32)],
    )(parts, diffusivity, sea_mask, own, *brought)
    north, south = shift(top, bottom, "lat")
    rim_lanes = -(-(quarters * members + 4) * HALO // LANES) * LANES
    rim = shape(height, rim_lanes)
    one, two, north, south = call(
        functools.partial(rim_kernel, width=width),
        (rim, rim, strip, strip),
        [pltpu.VMEM((height, rim_lanes), F32)] * 2,
    )(mid, north, south)
    one, two = exchange(one, two, ("lon", "mem"))
    lanes = members * span
    quarter = call(
        product_kernel,
        shape(quarters, rows // 2, 2 * width),
        [
            pltpu.VMEM((quarters, height, lanes), F32),
            pltpu.VMEM((2, quarters, height + 16, lanes), F32),
            pltpu.VMEM((5, height, lanes), F32),
            pltpu.VMEM((height, lanes), F32),
            pltpu.VMEM((4, height, LANES), F32),
            pltpu.VMEM((height, rim_lanes), F32),
            pltpu.VMEM((height, rim_lanes), F32),
        ],
    )(mid, north, south, one, two)
    quarter = lax.all_to_all(quarter, "mem", split_axis=0, concat_axis=0, tiled=True)
    increment, answers = call(
        answer_kernel, (shape(rows, cols), shape(places, SLOTS)), [pltpu.VMEM((LANES, places), F32)]
    )(quarter, turned)
    returned = lax.all_to_all(answers, tiles, split_axis=0, concat_axis=0, tiled=True)
    residual = call(
        residual_kernel, shape(chunks, LANES), [pltpu.VMEM((max(LANES, places), LANES), F32)]
    )(owner, rank, depart, returned)
    return increment, residual.reshape(chunks * LANES)


def solution(mesh):
    return jax.shard_map(
        per_device,
        mesh=mesh,
        in_specs=(
            P("mem", "lat", "lon"),
            P("lat", "lon"),
            P("lat", "lon"),
            P(("lat", "lon", "mem"), None),
            P(("lat", "lon", "mem")),
            P(("lat", "lon", "mem")),
            P(("lat", "lon", "mem")),
        ),
        out_specs=(P("lat", "lon"), P(("lat", "lon", "mem"))),
        check_vma=False,
    )
```

```python
import functools

import jax
import jax.numpy as jnp
from jax import lax
from jax.experimental import pallas as pl
from jax.experimental.pallas import tpu as pltpu
from jax.sharding import PartitionSpec as P

STEPS = 4
SLOTS = 32
HALO = 2 * STEPS
LANES = 128
F32 = jnp.float32
BF16 = jnp.bfloat16
I32 = jnp.int32

WHOLE = pl.BlockSpec(memory_space=pltpu.VMEM)
AWAY = pl.BlockSpec(memory_space=pl.ANY)


def call(kernel, outs, scratch=(), limit=24 << 20, place=WHOLE):
    def run(*operands):
        return pl.pallas_call(
            kernel,
            out_shape=outs,
            in_specs=[place] * len(operands),
            out_specs=jax.tree.map(lambda _: WHOLE, outs),
            scratch_shapes=list(scratch),
            compiler_params=pltpu.CompilerParams(vmem_limit_bytes=limit),
        )(*operands)

    return run


def halves(value):
    high = value.astype(BF16).astype(F32)
    return high, value - high


def nt_dot(a, b):
    return lax.dot_general(a, b, (((1,), (1,)), ((), ())), preferred_element_type=F32)


def bring(away_refs, near_refs, sem_ref):
    copies = [
        pltpu.make_async_copy(away, near, sem_ref.at[i])
        for i, (away, near) in enumerate(zip(away_refs, near_refs))
    ]
    for copy in copies:
        copy.start()
    for copy in copies:
        copy.wait()


def pack_kernel(*refs):
    out_ref, rank_ref = refs[4:6]
    owner_ref, cell_ref, depart_ref, weight_ref = refs[6:10]
    bring(refs[:4], refs[6:10], refs[10])
    places = out_ref.shape[0]
    chunks = owner_ref.shape[0]
    dest_ids = lax.broadcasted_iota(I32, (places, LANES), 0)
    slot_ids = lax.broadcasted_iota(I32, (SLOTS, LANES), 0).astype(F32)
    source = lax.broadcasted_iota(I32, (LANES, 2 * LANES), 0)
    target = lax.broadcasted_iota(I32, (LANES, 2 * LANES), 1)
    counter = jnp.where(source <= target, 1.0, 0.0).astype(BF16)
    seen = jnp.full((places, LANES), -1.0, F32)
    packed = jnp.zeros((places, 6 * SLOTS), F32)
    for j in range(chunks):
        hit = dest_ids == owner_ref[j : j + 1, :]
        names = jnp.where(hit, 1.0, 0.0).astype(BF16)
        counts = jnp.dot(names, counter, preferred_element_type=F32)
        rank = jnp.sum(jnp.where(hit, counts[:, :LANES] + seen, 0.0), axis=0, keepdims=True)
        seen = seen + counts[:, LANES:]
        rank_ref[j : j + 1, :] = rank
        weight = weight_ref[j : j + 1, :]
        product_high, product_low = halves(weight * depart_ref[j : j + 1, :])
        weight_high, weight_low = halves(weight)
        cell = cell_ref[j : j + 1, :]
        row = (cell // 256).astype(F32)
        col = (cell % 256).astype(F32)
        chosen = slot_ids == rank
        fields = [
            jnp.where(chosen, field, 0.0)
            for field in (product_high, weight_high, row, col, product_low, weight_low)
        ]
        packed = packed + nt_dot(names, jnp.concatenate(fields, axis=0).astype(BF16))
    low = jnp.concatenate(
        [packed[:, 4 * SLOTS :], jnp.zeros((places, 2 * SLOTS), F32)], axis=1
    )
    out_ref[...] = packed[:, : 4 * SLOTS] + low


def scatter_kernel(got_ref, near_ref, far_ref, out_ref, turned_ref, passed_ref):
    rows, cols = 64, 256
    passed_ref[0] = near_ref[...]
    passed_ref[1] = far_ref[1]
    turned_ref[...] = got_ref[...].T
    width = turned_ref.shape[1]
    row_ids = lax.broadcasted_iota(I32, (rows, width), 0).astype(F32)
    col_ids = lax.broadcasted_iota(I32, (cols, width), 0).astype(F32)
    total = jnp.zeros((4 * rows, cols), F32)
    for s in range(0, SLOTS, 2):
        left, right = [], []
        for k in (s, s + 1):
            product_high, product_low = halves(turned_ref[k : k + 1, :])
            weight_high, weight_low = halves(turned_ref[SLOTS + k : SLOTS + k + 1, :])
            in_row = row_ids == turned_ref[2 * SLOTS + k : 2 * SLOTS + k + 1, :]
            in_col = col_ids == turned_ref[3 * SLOTS + k : 3 * SLOTS + k + 1, :]
            left.append(
                jnp.concatenate(
                    [
                        jnp.where(in_row, v, 0.0)
                        for v in (product_high, product_low, weight_high, weight_low)
                    ],
                    axis=0,
                ).astype(BF16)
            )
            right.append(jnp.where(in_col, 1.0, 0.0).astype(BF16))
        total = total + nt_dot(jnp.concatenate(left, axis=1), jnp.concatenate(right, axis=1))
    product = total[:rows] + total[rows : 2 * rows]
    weight = total[2 * rows : 3 * rows] + total[3 * rows :]
    quarters, width = out_ref.shape[0], out_ref.shape[2] // 2
    for q in range(quarters):
        out_ref[q, :, :width] = product[:, q * width : (q + 1) * width]
        out_ref[q, :, width:] = weight[:, q * width : (q + 1) * width]


def quarter_kernel(members_ref, own_ref, near_ref, far_ref, kept_ref):
    members = members_ref.shape[0]
    quarters = kept_ref.shape[0]
    width = members_ref.shape[2] // quarters
    for k in range(members):
        value = members_ref[k].astype(F32)
        for q in range(quarters):
            kept_ref[q, :, k * width : (k + 1) * width] = value[:, q * width : (q + 1) * width]
    mine = lax.axis_index("mem")
    own_ref[...] = kept_ref[mine]
    near_ref[...] = kept_ref[mine ^ 1]
    far_ref[0] = kept_ref[mine ^ 2]
    far_ref[1] = kept_ref[mine ^ 3]


def reduce_kernel(parts_ref, rate_ref, sea_ref, *rest):
    quarters = parts_ref.shape[0]
    own_ref, far_ref, near_ref, mid_ref, top_ref, bottom_ref, kept_ref = rest
    piece_refs = (own_ref, near_ref.at[0], far_ref.at[0], near_ref.at[1])
    rows, lanes = own_ref.shape
    width = parts_ref.shape[2] // 2
    mine = lax.axis_index("mem")
    for k in range(quarters):
        mid_ref[mine ^ k, :, :lanes] = piece_refs[k][...]
    whole = parts_ref[0]
    for q in range(1, quarters):
        whole = whole + parts_ref[q]
    mid_ref[0, :, lanes:] = whole
    for q in range(quarters):
        at = slice(q * width, (q + 1) * width)
        kept_ref[q, :, :width] = rate_ref[:, at]
        kept_ref[q, :, width:] = sea_ref[:, at].astype(F32)
    mid_ref[1, :, lanes:] = kept_ref[mine]
    for q in range(quarters):
        size = lanes if q > 1 else lanes + 2 * width
        top_ref[q, :, :size] = mid_ref[q, :HALO, :size]
        bottom_ref[q, :, :size] = mid_ref[q, rows - HALO :, :size]
        if size < top_ref.shape[2]:
            top_ref[q, :, size:] = jnp.zeros((HALO, 2 * width), F32)
            bottom_ref[q, :, size:] = jnp.zeros((HALO, 2 * width), F32)


def fields_of(ref, width):
    quarters, lanes = ref.shape[0], ref.shape[2] - 2 * width
    places = [(q, k * width) for q in range(quarters) for k in range(lanes // width)]
    return places + [(0, lanes), (0, lanes + width), (1, lanes), (1, lanes + width)]


def rim_kernel(
    mid_ref, before_ref, after_ref, one_ref, two_ref, north_ref, south_ref, first_ref, last_ref, *, width
):
    rows, lanes = mid_ref.shape[1], mid_ref.shape[2]
    lat = lax.axis_index("lat")
    north_ref[...] = before_ref[...]
    south_ref[...] = after_ref[...]
    sea = slice(lanes - width, lanes)
    north_ref[1, :, sea] = jnp.where(lat == 0, 0.0, north_ref[1, :, sea])
    south_ref[1, :, sea] = jnp.where(lat == lax.axis_size("lat") - 1, 0.0, south_ref[1, :, sea])
    first_ref[...] = jnp.zeros(first_ref.shape, F32)
    last_ref[...] = jnp.zeros(last_ref.shape, F32)
    for k, (q, lane) in enumerate(fields_of(mid_ref, width)):
        at = slice(k * HALO, (k + 1) * HALO)
        for ref, cut in ((first_ref, lane), (last_ref, lane + width - HALO)):
            ref[:HALO, at] = north_ref[q, :, cut : cut + HALO]
            ref[HALO : HALO + rows, at] = mid_ref[q, :, cut : cut + HALO]
            ref[HALO + rows :, at] = south_ref[q, :, cut : cut + HALO]
    even = lax.axis_index("mem") % 2 == 0
    one_ref[...] = jnp.where(even, last_ref[...], first_ref[...])
    two_ref[...] = jnp.where(even, first_ref[...], last_ref[...])


def product_kernel(
    mid_ref, north_ref, south_ref, one_ref, two_ref, out_ref,
    members_ref, state_ref, weights_ref, tiled_ref, field_ref, west_ref, east_ref,
):
    groups, height, lanes = members_ref.shape
    rows = height - 2 * HALO
    width = out_ref.shape[2] // 2
    span = width + 2 * HALO
    windows = lanes // span
    divisor = groups * windows - 1
    pad = 8

    def tile_lanes(value):
        for k in range(windows):
            tiled_ref[:, k * span : (k + 1) * span] = value
        return tiled_ref[...]

    even = lax.axis_index("mem") % 2 == 0
    west_ref[...] = jnp.where(even, two_ref[...], one_ref[...])
    east_ref[...] = jnp.where(even, one_ref[...], two_ref[...])
    for k, (q, lane) in enumerate(fields_of(mid_ref, width)):
        rim = slice(k * HALO, (k + 1) * HALO)
        cut = slice(lane, lane + width)
        north, south = north_ref[q, :, cut], south_ref[q, :, cut]
        if k < groups * windows:
            ref, low = members_ref.at[k // windows], k % windows * span
        else:
            ref, low = field_ref.at[k - groups * windows], 0
        ref[:, low : low + HALO] = west_ref[:, rim]
        ref[:HALO, low + HALO : low + HALO + width] = north
        ref[HALO : HALO + rows, low + HALO : low + HALO + width] = mid_ref[q, :, cut]
        ref[HALO + rows :, low + HALO : low + HALO + width] = south
        ref[:, low + HALO + width : low + span] = east_ref[:, rim]
    innovation = field_ref[0, :, :span]
    weight_sum = field_ref[1, :, :span]
    sea_cover = field_ref[3, :, :span]

    rate = tile_lanes(field_ref[2, :, :span])
    sea = tile_lanes(sea_cover)
    north = 0.5 * (rate + pltpu.roll(rate, height - 1, 0)) * sea * pltpu.roll(sea, height - 1, 0)
    east = 0.5 * (rate + pltpu.roll(rate, lanes - 1, 1)) * sea * pltpu.roll(sea, lanes - 1, 1)
    south = pltpu.roll(north, 1, 0)
    west = pltpu.roll(east, 1, 1)
    weights_ref[0] = 1.0 - (north + south + east + west)
    weights_ref[1] = north
    weights_ref[2] = south
    weights_ref[3] = east
    weights_ref[4] = west
    state_ref[...] = jnp.zeros(state_ref.shape, F32)

    def sweep(source, target):
        for r in range(0, height, 8):
            centre_w, north_w, south_w, east_w, west_w = (
                weights_ref[i, r : r + 8, :] for i in range(5)
            )
            for g in range(groups):
                centre = state_ref[source, g, pad + r : pad + r + 8, :]
                above = state_ref[source, g, pad + r + 1 : pad + r + 9, :]
                below = state_ref[source, g, pad + r - 1 : pad + r + 7, :]
                state_ref[target, g, pad + r : pad + r + 8, :] = (
                    centre_w * centre
                    + (north_w * above + south_w * below)
                    + (east_w * pltpu.roll(centre, lanes - 1, 1) + west_w * pltpu.roll(centre, 1, 1))
                )

    def covariance(source):
        tiled = tile_lanes(source)
        for g in range(groups):
            state_ref[0, g, pad : pad + height, :] = members_ref[g] * tiled

        def pair(_, carry):
            sweep(0, 1)
            sweep(1, 0)
            return carry

        lax.fori_loop(0, STEPS // 2, pair, 0)
        total = members_ref[0] * state_ref[0, 0, pad : pad + height, :]
        for g in range(1, groups):
            total = total + members_ref[g] * state_ref[0, g, pad : pad + height, :]
        tiled_ref[...] = total
        summed = tiled_ref[:, :span]
        for k in range(1, windows):
            summed = summed + tiled_ref[:, k * span : (k + 1) * span]
        return sea_cover * summed / divisor

    first_pass = covariance(innovation)
    increment = covariance(innovation - weight_sum * first_pass)
    field_ref[0, :, :span] = increment
    half = (height - 2 * HALO) // 2
    for q in range(out_ref.shape[0]):
        out_ref[q, :, :width] = field_ref[0, HALO : HALO + half, HALO : HALO + width]
        out_ref[q, :, width:] = field_ref[0, HALO + half : HALO + 2 * half, HALO : HALO + width]


def answer_kernel(pieces_ref, turned_ref, tile_ref, out_ref, reply_ref):
    quarters, half, width = pieces_ref.shape[0], pieces_ref.shape[1], pieces_ref.shape[2] // 2
    rows, cols = tile_ref.shape
    for q in range(quarters):
        tile_ref[:half, q * width : (q + 1) * width] = pieces_ref[q, :, :width]
        tile_ref[half:, q * width : (q + 1) * width] = pieces_ref[q, :, width:]
    high, low = halves(tile_ref[...])
    both = jnp.concatenate([high, low], axis=0).astype(BF16)
    lanes = turned_ref.shape[1]
    row_ids = lax.broadcasted_iota(I32, (rows, lanes), 0).astype(F32)
    col_ids = lax.broadcasted_iota(I32, (cols, lanes), 0).astype(F32)
    reply_ref[...] = jnp.zeros(reply_ref.shape, F32)
    for k in range(SLOTS):
        in_row = row_ids == turned_ref[2 * SLOTS + k : 2 * SLOTS + k + 1, :]
        in_col = col_ids == turned_ref[3 * SLOTS + k : 3 * SLOTS + k + 1, :]
        picked = jnp.dot(both, jnp.where(in_col, 1.0, 0.0).astype(BF16), preferred_element_type=F32)
        picked = picked[:rows] + picked[rows:]
        reply_ref[k : k + 1, :] = jnp.sum(jnp.where(in_row, picked, 0.0), axis=0, keepdims=True)
    out_ref[...] = reply_ref[...].T[:, :SLOTS]


def residual_kernel(owner_ref, rank_ref, depart_ref, got_ref, out_ref, wide_ref):
    places = got_ref.shape[0]
    chunks = owner_ref.shape[0]
    wide_ref[...] = jnp.zeros(wide_ref.shape, F32)
    wide_ref[:places, :SLOTS] = got_ref[...]
    turned = wide_ref[...].T[:SLOTS, :]
    high, low = halves(turned)
    both = jnp.concatenate([high, low], axis=0).astype(BF16)
    dest_ids = lax.broadcasted_iota(I32, (wide_ref.shape[0], LANES), 0)
    slot_ids = lax.broadcasted_iota(I32, (SLOTS, LANES), 0).astype(F32)
    for j in range(chunks):
        names = jnp.where(dest_ids == owner_ref[j : j + 1, :], 1.0, 0.0).astype(BF16)
        picked = jnp.dot(both, names, preferred_element_type=F32)
        picked = picked[:SLOTS] + picked[SLOTS:]
        value = jnp.sum(
            jnp.where(slot_ids == rank_ref[j : j + 1, :], picked, 0.0), axis=0, keepdims=True
        )
        out_ref[j : j + 1, :] = depart_ref[j : j + 1, :] - value


def shape(*dims, dtype=F32):
    return jax.ShapeDtypeStruct(dims, dtype)


def shift(first, last, axis):
    size = lax.axis_size(axis)
    up = [(i, (i + 1) % size) for i in range(size)]
    return lax.ppermute(last, axis, up), lax.ppermute(first, axis, [(j, i) for i, j in up])


def exchange(first, second, axes):
    size = 1
    for axis in axes:
        size *= lax.axis_size(axis)
    swaps = [[(i + k, (i + k + 1) % size) for i in range(0, size, 2)] for k in range(2)]
    both = [pairs + [(j, i) for i, j in pairs] for pairs in swaps]
    return lax.ppermute(first, axes, both[0]), lax.ppermute(second, axes, both[1])


def per_device(perturbations, diffusivity, sea_mask, obs_owner, obs_cell, obs_depart, obs_weight):
    members, rows, cols = perturbations.shape
    quarters = lax.axis_size("mem")
    places = lax.axis_size("lat") * lax.axis_size("lon")
    width = cols // quarters
    span = width + 2 * HALO
    height = rows + 2 * HALO
    chunks = obs_cell.shape[0] // LANES
    owner, cell, depart, weight = (
        a.reshape(chunks, LANES) for a in (obs_owner, obs_cell, obs_depart, obs_weight)
    )
    tiles = ("lat", "lon")

    piece = shape(rows, members * width)
    pair = shape(2, rows, members * width)
    own, near, far = call(
        quarter_kernel, (piece, piece, pair), [pltpu.VMEM((quarters, rows, members * width), F32)]
    )(perturbations)
    outgoing, rank = call(
        pack_kernel,
        (shape(places, LANES), shape(chunks, LANES)),
        [pltpu.VMEM((chunks, LANES), a.dtype) for a in (owner, cell, depart, weight)]
        + [pltpu.SemaphoreType.DMA((4,))],
        place=AWAY,
    )(owner, cell, depart, weight)
    got = lax.all_to_all(outgoing, tiles, split_axis=0, concat_axis=0, tiled=True)
    far = lax.ppermute(far, "mem", [(i, i ^ 2) for i in range(quarters)])
    got, far = lax.optimization_barrier((got, far))

    parts, turned, passed = call(
        scatter_kernel, (shape(quarters, rows, 2 * width), shape(LANES, places), pair)
    )(got, near, far)
    near = lax.ppermute(passed, "mem", [(i, i ^ 1) for i in range(quarters)])
    parts = lax.all_to_all(parts, "mem", split_axis=0, concat_axis=0, tiled=True)
    field_lanes = members * width + 2 * width
    strip = shape(quarters, HALO, field_lanes)
    mid, top, bottom = call(
        reduce_kernel,
        (shape(quarters, rows, field_lanes), strip, strip),
        [pltpu.VMEM((quarters, rows, 2 * width), F32)],
    )(parts, diffusivity, sea_mask, own, far, near)
    north, south = shift(top, bottom, "lat")
    rim_lanes = -(-(quarters * members + 4) * HALO // LANES) * LANES
    rim = shape(height, rim_lanes)
    one, two, north, south = call(
        functools.partial(rim_kernel, width=width),
        (rim, rim, strip, strip),
        [pltpu.VMEM((height, rim_lanes), F32)] * 2,
    )(mid, north, south)
    one, two = exchange(one, two, ("lon", "mem"))
    lanes = members * span
    quarter = call(
        product_kernel,
        shape(quarters, rows // 2, 2 * width),
        [
            pltpu.VMEM((quarters, height, lanes), F32),
            pltpu.VMEM((2, quarters, height + 16, lanes), F32),
            pltpu.VMEM((5, height, lanes), F32),
            pltpu.VMEM((height, lanes), F32),
            pltpu.VMEM((4, height, LANES), F32),
            pltpu.VMEM((height, rim_lanes), F32),
            pltpu.VMEM((height, rim_lanes), F32),
        ],
    )(mid, north, south, one, two)
    quarter = lax.all_to_all(quarter, "mem", split_axis=0, concat_axis=0, tiled=True)
    increment, answers = call(
        answer_kernel, (shape(rows, cols), shape(places, SLOTS)), [pltpu.VMEM((LANES, places), F32)]
    )(quarter, turned)
    returned = lax.all_to_all(answers, tiles, split_axis=0, concat_axis=0, tiled=True)
    residual = call(
        residual_kernel, shape(chunks, LANES), [pltpu.VMEM((max(LANES, places), LANES), F32)]
    )(owner, rank, depart, returned)
    return increment, residual.reshape(chunks * LANES)


def solution(mesh):
    return jax.shard_map(
        per_device,
        mesh=mesh,
        in_specs=(
            P("mem", "lat", "lon"),
            P("lat", "lon"),
            P("lat", "lon"),
            P(("lat", "lon", "mem"), None),
            P(("lat", "lon", "mem")),
            P(("lat", "lon", "mem")),
            P(("lat", "lon", "mem")),
        ),
        out_specs=(P("lat", "lon"), P(("lat", "lon", "mem"))),
        check_vma=False,
    )
```

```python
import functools

import jax
import jax.numpy as jnp
from jax import lax
from jax.experimental import pallas as pl
from jax.experimental.pallas import tpu as pltpu
from jax.sharding import PartitionSpec as P

STEPS = 4
SLOTS = 32
HALO = 2 * STEPS
LANES = 128
F32 = jnp.float32
BF16 = jnp.bfloat16
I32 = jnp.int32

WHOLE = pl.BlockSpec(memory_space=pltpu.VMEM)
AWAY = pl.BlockSpec(memory_space=pl.ANY)


def call(kernel, outs, scratch=(), limit=24 << 20, place=WHOLE):
    def run(*operands):
        return pl.pallas_call(
            kernel,
            out_shape=outs,
            in_specs=[place] * len(operands),
            out_specs=jax.tree.map(lambda _: WHOLE, outs),
            scratch_shapes=list(scratch),
            compiler_params=pltpu.CompilerParams(vmem_limit_bytes=limit),
        )(*operands)

    return run


def halves(value):
    high = value.astype(BF16).astype(F32)
    return high, value - high


def nt_dot(a, b):
    return lax.dot_general(a, b, (((1,), (1,)), ((), ())), preferred_element_type=F32)


def bring(away_refs, near_refs, sem_ref):
    copies = [
        pltpu.make_async_copy(away, near, sem_ref.at[i])
        for i, (away, near) in enumerate(zip(away_refs, near_refs))
    ]
    for copy in copies:
        copy.start()
    for copy in copies:
        copy.wait()


def pack_kernel(*refs):
    out_ref, rank_ref = refs[4:6]
    owner_ref, cell_ref, depart_ref, weight_ref = refs[6:10]
    bring(refs[:4], refs[6:10], refs[10])
    places = out_ref.shape[0]
    chunks = owner_ref.shape[0]
    dest_ids = lax.broadcasted_iota(I32, (places, LANES), 0)
    slot_ids = lax.broadcasted_iota(I32, (SLOTS, LANES), 0).astype(F32)
    source = lax.broadcasted_iota(I32, (LANES, 2 * LANES), 0)
    target = lax.broadcasted_iota(I32, (LANES, 2 * LANES), 1)
    counter = jnp.where(source <= target, 1.0, 0.0).astype(BF16)
    seen = jnp.full((places, LANES), -1.0, F32)
    packed = jnp.zeros((places, 6 * SLOTS), F32)
    for j in range(chunks):
        hit = dest_ids == owner_ref[j : j + 1, :]
        names = jnp.where(hit, 1.0, 0.0).astype(BF16)
        counts = jnp.dot(names, counter, preferred_element_type=F32)
        rank = jnp.sum(jnp.where(hit, counts[:, :LANES] + seen, 0.0), axis=0, keepdims=True)
        seen = seen + counts[:, LANES:]
        rank_ref[j : j + 1, :] = rank
        weight = weight_ref[j : j + 1, :]
        product_high, product_low = halves(weight * depart_ref[j : j + 1, :])
        weight_high, weight_low = halves(weight)
        cell = cell_ref[j : j + 1, :]
        row = (cell // 256).astype(F32)
        col = (cell % 256).astype(F32)
        chosen = slot_ids == rank
        fields = [
            jnp.where(chosen, field, 0.0)
            for field in (product_high, weight_high, row, col, product_low, weight_low)
        ]
        packed = packed + nt_dot(names, jnp.concatenate(fields, axis=0).astype(BF16))
    low = jnp.concatenate(
        [packed[:, 4 * SLOTS :], jnp.zeros((places, 2 * SLOTS), F32)], axis=1
    )
    out_ref[...] = packed[:, : 4 * SLOTS] + low


def scatter_kernel(got_ref, near_ref, far_ref, out_ref, turned_ref, passed_ref, wide_ref):
    rows, cols = 64, 256
    passed_ref[0] = near_ref[...]
    passed_ref[1] = far_ref[1]
    turned_ref[...] = got_ref[...].T
    width = turned_ref.shape[1]
    row_ids = lax.broadcasted_iota(I32, (rows, width), 0).astype(F32)
    col_ids = lax.broadcasted_iota(I32, (cols, width), 0).astype(F32)
    total = jnp.zeros((4 * rows, cols), F32)
    for s in range(0, SLOTS, 2):
        left, right = [], []
        for k in (s, s + 1):
            product_high, product_low = halves(turned_ref[k : k + 1, :])
            weight_high, weight_low = halves(turned_ref[SLOTS + k : SLOTS + k + 1, :])
            in_row = row_ids == turned_ref[2 * SLOTS + k : 2 * SLOTS + k + 1, :]
            in_col = col_ids == turned_ref[3 * SLOTS + k : 3 * SLOTS + k + 1, :]
            left.append(
                jnp.concatenate(
                    [
                        jnp.where(in_row, v, 0.0)
                        for v in (product_high, product_low, weight_high, weight_low)
                    ],
                    axis=0,
                ).astype(BF16)
            )
            right.append(jnp.where(in_col, 1.0, 0.0).astype(BF16))
        total = total + nt_dot(jnp.concatenate(left, axis=1), jnp.concatenate(right, axis=1))
    product = total[:rows] + total[rows : 2 * rows]
    weight = total[2 * rows : 3 * rows] + total[3 * rows :]
    quarters = out_ref.shape[0]
    width = cols // quarters
    wide_ref[...] = jnp.zeros(wide_ref.shape, F32)
    for f, field in enumerate((product, weight)):
        wide_ref[f, :, HALO : HALO + cols] = field
        for q in range(quarters):
            out_ref[q, :rows, f * width : (f + 1) * width] = field[:, q * width : (q + 1) * width]
            low, high = q * width, (q + 1) * width + HALO
            for b in range(4):
                block, lane = slice(16 * b, 16 * (b + 1)), 32 * b + 2 * HALO * f
                out_ref[q, rows:, lane : lane + HALO] = wide_ref[f, block, low : low + HALO]
                out_ref[q, rows:, lane + HALO : lane + 2 * HALO] = wide_ref[f, block, high : high + HALO]


def cut_quarters(value, wide_ref, kept_ref, low):
    quarters, cols = kept_ref.shape[0], value.shape[1]
    width = cols // quarters
    span = width + 2 * HALO
    wide_ref[:, HALO : HALO + cols] = value
    for q in range(quarters):
        kept_ref[q, :, low : low + span] = wide_ref[:, q * width : q * width + span]


def quarter_kernel(members_ref, own_ref, near_ref, far_ref, kept_ref, wide_ref):
    members = members_ref.shape[0]
    span = kept_ref.shape[2] // members
    wide_ref[...] = jnp.zeros(wide_ref.shape, F32)
    for k in range(members):
        cut_quarters(members_ref[k].astype(F32), wide_ref, kept_ref, k * span)
    mine = lax.axis_index("mem")
    own_ref[...] = kept_ref[mine]
    near_ref[...] = kept_ref[mine ^ 1]
    far_ref[0] = kept_ref[mine ^ 2]
    far_ref[1] = kept_ref[mine ^ 3]


def reduce_kernel(parts_ref, rate_ref, sea_ref, *rest):
    quarters = parts_ref.shape[0]
    own_ref, far_ref, near_ref, mid_ref, top_ref, bottom_ref, kept_ref, wide_ref, whole_ref = rest
    piece_refs = (own_ref, near_ref.at[0], far_ref.at[0], near_ref.at[1])
    rows, lanes = own_ref.shape
    width = rate_ref.shape[1] // quarters
    span = width + 2 * HALO
    mine = lax.axis_index("mem")
    mid_ref[:, :, lanes:] = jnp.zeros((quarters, rows, mid_ref.shape[2] - lanes), F32)
    for k in range(quarters):
        mid_ref[mine ^ k, :, :lanes] = piece_refs[k][...]
    whole = parts_ref[0]
    for q in range(1, quarters):
        whole = whole + parts_ref[q]
    whole_ref[...] = whole
    for f in range(2):
        low = lanes + f * span
        mid_ref[0, :, low + HALO : low + HALO + width] = whole_ref[:rows, f * width : (f + 1) * width]
        for b in range(4):
            block, lane = slice(16 * b, 16 * (b + 1)), 32 * b + 2 * HALO * f
            mid_ref[0, block, low : low + HALO] = whole_ref[rows:, lane : lane + HALO]
            mid_ref[0, block, low + HALO + width : low + span] = whole_ref[rows:, lane + HALO : lane + 2 * HALO]
    wide_ref[...] = jnp.zeros(wide_ref.shape, F32)
    cut_quarters(rate_ref[...], wide_ref, kept_ref, 0)
    cut_quarters(sea_ref[...].astype(F32), wide_ref, kept_ref, span)
    mid_ref[1, :, lanes : lanes + 2 * span] = kept_ref[mine, :, : 2 * span]
    for q in range(quarters):
        top_ref[q] = mid_ref[q, :HALO, :]
        bottom_ref[q] = mid_ref[q, rows - HALO :, :]


def fields_of(quarters, lanes, span):
    places = [(q, k) for q in range(quarters) for k in range(0, lanes, span)]
    return places + [(0, lanes), (0, lanes + span), (1, lanes), (1, lanes + span)]


def rim_kernel(mid_ref, before_ref, after_ref, out_ref, north_ref, south_ref, *, lanes, span):
    quarters, rows = mid_ref.shape[:2]
    lat, mine = lax.axis_index("lat"), lax.axis_index("mem")
    north_ref[...] = before_ref[...]
    south_ref[...] = after_ref[...]
    sea = slice(lanes + span, lanes + 2 * span)
    north_ref[1, :, sea] = jnp.where(lat == 0, 0.0, north_ref[1, :, sea])
    south_ref[1, :, sea] = jnp.where(lat == lax.axis_size("lat") - 1, 0.0, south_ref[1, :, sea])
    out_ref[...] = jnp.zeros(out_ref.shape, F32)
    for edge, offset in ((0, HALO), (quarters - 1, span - 2 * HALO)):

        @pl.when(mine == edge)
        def _():
            for k, (q, lane) in enumerate(fields_of(quarters, lanes, span)):
                at, cut = slice(k * HALO, (k + 1) * HALO), slice(lane + offset, lane + offset + HALO)
                out_ref[:HALO, at] = north_ref[q, :, cut]
                out_ref[HALO : HALO + rows, at] = mid_ref[q, :, cut]
                out_ref[HALO + rows :, at] = south_ref[q, :, cut]


def product_kernel(
    mid_ref, north_ref, south_ref, got_ref, out_ref,
    members_ref, state_ref, weights_ref, tiled_ref, field_ref,
):
    groups, height, lanes = members_ref.shape
    rows = height - 2 * HALO
    width = out_ref.shape[2] // 2
    span = width + 2 * HALO
    windows = lanes // span
    divisor = groups * windows - 1
    pad = 8

    def tile_lanes(value):
        for k in range(windows):
            tiled_ref[:, k * span : (k + 1) * span] = value
        return tiled_ref[...]

    inner = slice(HALO, HALO + rows)
    for g in range(groups):
        for part_ref, at in ((north_ref, slice(0, HALO)), (mid_ref, inner), (south_ref, slice(HALO + rows, height))):
            members_ref[g, at, :] = part_ref[g, :, :lanes]
            if g < 2:
                for f in range(2):
                    low = lanes + f * span
                    field_ref[2 * g + f, at, :span] = part_ref[g, :, low : low + span]
    mine = lax.axis_index("mem")
    for edge, offset in ((0, 0), (lax.axis_size("mem") - 1, span - HALO)):

        @pl.when(mine == edge)
        def _():
            for k in range(groups * windows + 4):
                other = k - groups * windows
                ref = members_ref.at[k // windows] if other < 0 else field_ref.at[other]
                low = (k % windows * span if other < 0 else 0) + offset
                ref[:, low : low + HALO] = got_ref[:, k * HALO : (k + 1) * HALO]

    innovation = field_ref[0, :, :span]
    weight_sum = field_ref[1, :, :span]
    sea_cover = field_ref[3, :, :span]

    rate = tile_lanes(field_ref[2, :, :span])
    sea = tile_lanes(sea_cover)
    north = 0.5 * (rate + pltpu.roll(rate, height - 1, 0)) * sea * pltpu.roll(sea, height - 1, 0)
    east = 0.5 * (rate + pltpu.roll(rate, lanes - 1, 1)) * sea * pltpu.roll(sea, lanes - 1, 1)
    south = pltpu.roll(north, 1, 0)
    west = pltpu.roll(east, 1, 1)
    weights_ref[0] = 1.0 - (north + south + east + west)
    weights_ref[1] = north
    weights_ref[2] = south
    weights_ref[3] = east
    weights_ref[4] = west
    state_ref[...] = jnp.zeros(state_ref.shape, F32)

    def sweep(source, target):
        for r in range(0, height, 8):
            centre_w, north_w, south_w, east_w, west_w = (
                weights_ref[i, r : r + 8, :] for i in range(5)
            )
            for g in range(groups):
                centre = state_ref[source, g, pad + r : pad + r + 8, :]
                above = state_ref[source, g, pad + r + 1 : pad + r + 9, :]
                below = state_ref[source, g, pad + r - 1 : pad + r + 7, :]
                state_ref[target, g, pad + r : pad + r + 8, :] = (
                    centre_w * centre
                    + (north_w * above + south_w * below)
                    + (east_w * pltpu.roll(centre, lanes - 1, 1) + west_w * pltpu.roll(centre, 1, 1))
                )

    def covariance(source):
        tiled = tile_lanes(source)
        for g in range(groups):
            state_ref[0, g, pad : pad + height, :] = members_ref[g] * tiled

        def pair(_, carry):
            sweep(0, 1)
            sweep(1, 0)
            return carry

        lax.fori_loop(0, STEPS // 2, pair, 0)
        total = members_ref[0] * state_ref[0, 0, pad : pad + height, :]
        for g in range(1, groups):
            total = total + members_ref[g] * state_ref[0, g, pad : pad + height, :]
        tiled_ref[...] = total
        summed = tiled_ref[:, :span]
        for k in range(1, windows):
            summed = summed + tiled_ref[:, k * span : (k + 1) * span]
        return sea_cover * summed / divisor

    first_pass = covariance(innovation)
    increment = covariance(innovation - weight_sum * first_pass)
    field_ref[0, :, :span] = increment
    half = (height - 2 * HALO) // 2
    for q in range(out_ref.shape[0]):
        out_ref[q, :, :width] = field_ref[0, HALO : HALO + half, HALO : HALO + width]
        out_ref[q, :, width:] = field_ref[0, HALO + half : HALO + 2 * half, HALO : HALO + width]


def answer_kernel(pieces_ref, turned_ref, tile_ref, out_ref, reply_ref):
    quarters, half, width = pieces_ref.shape[0], pieces_ref.shape[1], pieces_ref.shape[2] // 2
    rows, cols = tile_ref.shape
    for q in range(quarters):
        tile_ref[:half, q * width : (q + 1) * width] = pieces_ref[q, :, :width]
        tile_ref[half:, q * width : (q + 1) * width] = pieces_ref[q, :, width:]
    high, low = halves(tile_ref[...])
    both = jnp.concatenate([high, low], axis=0).astype(BF16)
    lanes = turned_ref.shape[1]
    row_ids = lax.broadcasted_iota(I32, (rows, lanes), 0).astype(F32)
    col_ids = lax.broadcasted_iota(I32, (cols, lanes), 0).astype(F32)
    reply_ref[...] = jnp.zeros(reply_ref.shape, F32)
    for k in range(SLOTS):
        in_row = row_ids == turned_ref[2 * SLOTS + k : 2 * SLOTS + k + 1, :]
        in_col = col_ids == turned_ref[3 * SLOTS + k : 3 * SLOTS + k + 1, :]
        picked = jnp.dot(both, jnp.where(in_col, 1.0, 0.0).astype(BF16), preferred_element_type=F32)
        picked = picked[:rows] + picked[rows:]
        reply_ref[k : k + 1, :] = jnp.sum(jnp.where(in_row, picked, 0.0), axis=0, keepdims=True)
    out_ref[...] = reply_ref[...].T[:, :SLOTS]


def residual_kernel(owner_ref, rank_ref, depart_ref, got_ref, out_ref, wide_ref):
    places = got_ref.shape[0]
    chunks = owner_ref.shape[0]
    wide_ref[...] = jnp.zeros(wide_ref.shape, F32)
    wide_ref[:places, :SLOTS] = got_ref[...]
    turned = wide_ref[...].T[:SLOTS, :]
    high, low = halves(turned)
    both = jnp.concatenate([high, low], axis=0).astype(BF16)
    dest_ids = lax.broadcasted_iota(I32, (wide_ref.shape[0], LANES), 0)
    slot_ids = lax.broadcasted_iota(I32, (SLOTS, LANES), 0).astype(F32)
    for j in range(chunks):
        names = jnp.where(dest_ids == owner_ref[j : j + 1, :], 1.0, 0.0).astype(BF16)
        picked = jnp.dot(both, names, preferred_element_type=F32)
        picked = picked[:SLOTS] + picked[SLOTS:]
        value = jnp.sum(
            jnp.where(slot_ids == rank_ref[j : j + 1, :], picked, 0.0), axis=0, keepdims=True
        )
        out_ref[j : j + 1, :] = depart_ref[j : j + 1, :] - value


def shape(*dims, dtype=F32):
    return jax.ShapeDtypeStruct(dims, dtype)


def shift(first, last, axis):
    size = lax.axis_size(axis)
    up = [(i, (i + 1) % size) for i in range(size)]
    return lax.ppermute(last, axis, up), lax.ppermute(first, axis, [(j, i) for i, j in up])


def per_device(perturbations, diffusivity, sea_mask, obs_owner, obs_cell, obs_depart, obs_weight):
    members, rows, cols = perturbations.shape
    quarters = lax.axis_size("mem")
    places = lax.axis_size("lat") * lax.axis_size("lon")
    width = cols // quarters
    span = width + 2 * HALO
    height = rows + 2 * HALO
    chunks = obs_cell.shape[0] // LANES
    owner, cell, depart, weight = (
        a.reshape(chunks, LANES) for a in (obs_owner, obs_cell, obs_depart, obs_weight)
    )
    tiles = ("lat", "lon")

    lanes = members * span
    piece = shape(rows, lanes)
    pair = shape(2, rows, lanes)
    wide = pltpu.VMEM((rows, cols + LANES), F32)
    own, near, far = call(
        quarter_kernel, (piece, piece, pair), [pltpu.VMEM((quarters, rows, lanes), F32), wide]
    )(perturbations)
    outgoing, rank = call(
        pack_kernel,
        (shape(places, LANES), shape(chunks, LANES)),
        [pltpu.VMEM((chunks, LANES), a.dtype) for a in (owner, cell, depart, weight)]
        + [pltpu.SemaphoreType.DMA((4,))],
        place=AWAY,
    )(owner, cell, depart, weight)
    got = lax.all_to_all(outgoing, tiles, split_axis=0, concat_axis=0, tiled=True)
    far = lax.ppermute(far, "mem", [(i, i ^ 2) for i in range(quarters)])
    got, far = lax.optimization_barrier((got, far))

    parts, turned, passed = call(
        scatter_kernel,
        (shape(quarters, rows + 2 * HALO, 2 * width), shape(LANES, places), pair),
        [pltpu.VMEM((2, rows, cols + LANES), F32)],
    )(got, near, far)
    near = lax.ppermute(passed, "mem", [(i, i ^ 1) for i in range(quarters)])
    parts = lax.all_to_all(parts, "mem", split_axis=0, concat_axis=0, tiled=True)
    field_lanes = lanes + 2 * LANES
    strip = shape(quarters, HALO, field_lanes)
    mid, top, bottom = call(
        reduce_kernel,
        (shape(quarters, rows, field_lanes), strip, strip),
        [
            pltpu.VMEM((quarters, rows, 2 * LANES), F32),
            wide,
            pltpu.VMEM((rows + 2 * HALO, 2 * width), F32),
        ],
    )(parts, diffusivity, sea_mask, own, far, near)
    north, south = shift(top, bottom, "lat")
    rim_lanes = -(-(quarters * members + 4) * HALO // LANES) * LANES
    edge, north, south = call(
        functools.partial(rim_kernel, lanes=lanes, span=span),
        (shape(height, rim_lanes), strip, strip),
    )(mid, north, south)
    devices = lax.axis_size("lon") * quarters
    ends = [(i - 1, i % devices) for i in range(quarters, devices + 1, quarters)]
    got = lax.ppermute(edge, ("lon", "mem"), ends + [(j, i) for i, j in ends])
    quarter = call(
        product_kernel,
        shape(quarters, rows // 2, 2 * width),
        [
            pltpu.VMEM((quarters, height, lanes), F32),
            pltpu.VMEM((2, quarters, height + 16, lanes), F32),
            pltpu.VMEM((5, height, lanes), F32),
            pltpu.VMEM((height, lanes), F32),
            pltpu.VMEM((4, height, LANES), F32),
        ],
    )(mid, north, south, got)
    quarter = lax.all_to_all(quarter, "mem", split_axis=0, concat_axis=0, tiled=True)
    increment, answers = call(
        answer_kernel, (shape(rows, cols), shape(places, SLOTS)), [pltpu.VMEM((LANES, places), F32)]
    )(quarter, turned)
    returned = lax.all_to_all(answers, tiles, split_axis=0, concat_axis=0, tiled=True)
    residual = call(
        residual_kernel, shape(chunks, LANES), [pltpu.VMEM((max(LANES, places), LANES), F32)]
    )(owner, rank, depart, returned)
    return increment, residual.reshape(chunks * LANES)


def solution(mesh):
    return jax.shard_map(
        per_device,
        mesh=mesh,
        in_specs=(
            P("mem", "lat", "lon"),
            P("lat", "lon"),
            P("lat", "lon"),
            P(("lat", "lon", "mem"), None),
            P(("lat", "lon", "mem")),
            P(("lat", "lon", "mem")),
            P(("lat", "lon", "mem")),
        ),
        out_specs=(P("lat", "lon"), P(("lat", "lon", "mem"))),
        check_vma=False,
    )
```

```python
import functools

import jax
import jax.numpy as jnp
from jax import lax
from jax.experimental import pallas as pl
from jax.experimental.pallas import tpu as pltpu
from jax.sharding import PartitionSpec as P

STEPS = 4
SLOTS = 32
HALO = 2 * STEPS
LANES = 128
F32 = jnp.float32
BF16 = jnp.bfloat16
I32 = jnp.int32

WHOLE = pl.BlockSpec(memory_space=pltpu.VMEM)
AWAY = pl.BlockSpec(memory_space=pl.ANY)


def call(kernel, outs, scratch=(), limit=24 << 20, place=WHOLE):
    def run(*operands):
        return pl.pallas_call(
            kernel,
            out_shape=outs,
            in_specs=[place] * len(operands),
            out_specs=jax.tree.map(lambda _: WHOLE, outs),
            scratch_shapes=list(scratch),
            compiler_params=pltpu.CompilerParams(vmem_limit_bytes=limit),
        )(*operands)

    return run


def halves(value):
    high = value.astype(BF16).astype(F32)
    return high, value - high


def nt_dot(a, b):
    return lax.dot_general(a, b, (((1,), (1,)), ((), ())), preferred_element_type=F32)


def bring(away_refs, near_refs, sem_ref):
    copies = [
        pltpu.make_async_copy(away, near, sem_ref.at[i])
        for i, (away, near) in enumerate(zip(away_refs, near_refs))
    ]
    for copy in copies:
        copy.start()
    for copy in copies:
        copy.wait()


def pack_kernel(*refs):
    out_ref, rank_ref = refs[4:6]
    owner_ref, cell_ref, depart_ref, weight_ref = refs[6:10]
    bring(refs[:4], refs[6:10], refs[10])
    places = out_ref.shape[0]
    chunks = owner_ref.shape[0]
    dest_ids = lax.broadcasted_iota(I32, (places, LANES), 0)
    slot_ids = lax.broadcasted_iota(I32, (SLOTS, LANES), 0).astype(F32)
    source = lax.broadcasted_iota(I32, (LANES, 2 * LANES), 0)
    target = lax.broadcasted_iota(I32, (LANES, 2 * LANES), 1)
    counter = jnp.where(source <= target, 1.0, 0.0).astype(BF16)
    seen = jnp.full((places, LANES), -1.0, F32)
    packed = jnp.zeros((places, 6 * SLOTS), F32)
    for j in range(chunks):
        hit = dest_ids == owner_ref[j : j + 1, :]
        names = jnp.where(hit, 1.0, 0.0).astype(BF16)
        counts = jnp.dot(names, counter, preferred_element_type=F32)
        rank = jnp.sum(jnp.where(hit, counts[:, :LANES] + seen, 0.0), axis=0, keepdims=True)
        seen = seen + counts[:, LANES:]
        rank_ref[j : j + 1, :] = rank
        weight = weight_ref[j : j + 1, :]
        product_high, product_low = halves(weight * depart_ref[j : j + 1, :])
        weight_high, weight_low = halves(weight)
        cell = cell_ref[j : j + 1, :]
        row = (cell // 256).astype(F32)
        col = (cell % 256).astype(F32)
        chosen = slot_ids == rank
        fields = [
            jnp.where(chosen, field, 0.0)
            for field in (product_high, weight_high, row, col, product_low, weight_low)
        ]
        packed = packed + nt_dot(names, jnp.concatenate(fields, axis=0).astype(BF16))
    low = jnp.concatenate(
        [packed[:, 4 * SLOTS :], jnp.zeros((places, 2 * SLOTS), F32)], axis=1
    )
    out_ref[...] = packed[:, : 4 * SLOTS] + low


def scatter_kernel(got_ref, near_ref, far_ref, out_ref, turned_ref, passed_ref, wide_ref):
    rows, cols = 64, 256
    passed_ref[0] = near_ref[...]
    passed_ref[1] = far_ref[1]
    turned_ref[...] = got_ref[...].T
    width = turned_ref.shape[1]
    row_ids = lax.broadcasted_iota(I32, (rows, width), 0).astype(F32)
    col_ids = lax.broadcasted_iota(I32, (cols, width), 0).astype(F32)
    total = jnp.zeros((4 * rows, cols), F32)
    for s in range(0, SLOTS, 2):
        left, right = [], []
        for k in (s, s + 1):
            product_high, product_low = halves(turned_ref[k : k + 1, :])
            weight_high, weight_low = halves(turned_ref[SLOTS + k : SLOTS + k + 1, :])
            in_row = row_ids == turned_ref[2 * SLOTS + k : 2 * SLOTS + k + 1, :]
            in_col = col_ids == turned_ref[3 * SLOTS + k : 3 * SLOTS + k + 1, :]
            left.append(
                jnp.concatenate(
                    [
                        jnp.where(in_row, v, 0.0)
                        for v in (product_high, product_low, weight_high, weight_low)
                    ],
                    axis=0,
                ).astype(BF16)
            )
            right.append(jnp.where(in_col, 1.0, 0.0).astype(BF16))
        total = total + nt_dot(jnp.concatenate(left, axis=1), jnp.concatenate(right, axis=1))
    product = total[:rows] + total[rows : 2 * rows]
    weight = total[2 * rows : 3 * rows] + total[3 * rows :]
    quarters = out_ref.shape[0]
    width = cols // quarters
    wide_ref[...] = jnp.zeros(wide_ref.shape, F32)
    for f, field in enumerate((product, weight)):
        wide_ref[f, :, HALO : HALO + cols] = field
        for q in range(quarters):
            out_ref[q, :rows, f * width : (f + 1) * width] = field[:, q * width : (q + 1) * width]
            low, high = q * width, (q + 1) * width + HALO
            for b in range(4):
                block, lane = slice(16 * b, 16 * (b + 1)), 32 * b + 2 * HALO * f
                out_ref[q, rows:, lane : lane + HALO] = wide_ref[f, block, low : low + HALO]
                out_ref[q, rows:, lane + HALO : lane + 2 * HALO] = wide_ref[f, block, high : high + HALO]


def cut_quarters(value, wide_ref, kept_ref, low):
    quarters, cols = kept_ref.shape[0], value.shape[1]
    width = cols // quarters
    span = width + 2 * HALO
    wide_ref[:, HALO : HALO + cols] = value
    for q in range(quarters):
        kept_ref[q, :, low : low + span] = wide_ref[:, q * width : q * width + span]


def quarter_kernel(members_ref, own_ref, near_ref, far_ref, kept_ref, wide_ref):
    members = members_ref.shape[0]
    span = kept_ref.shape[2] // members
    wide_ref[...] = jnp.zeros(wide_ref.shape, F32)
    for k in range(members):
        cut_quarters(members_ref[k].astype(F32), wide_ref, kept_ref, k * span)
    mine = lax.axis_index("mem")
    own_ref[...] = kept_ref[mine]
    near_ref[...] = kept_ref[mine ^ 1]
    far_ref[0] = kept_ref[mine ^ 2]
    far_ref[1] = kept_ref[mine ^ 3]


def reduce_kernel(parts_ref, rate_ref, sea_ref, *rest):
    quarters = parts_ref.shape[0]
    own_ref, far_ref, near_ref, mid_ref, out_ref, kept_ref, wide_ref, whole_ref = rest
    piece_refs = (own_ref, near_ref.at[0], far_ref.at[0], near_ref.at[1])
    rows, lanes = own_ref.shape
    width = rate_ref.shape[1] // quarters
    span = width + 2 * HALO
    mine = lax.axis_index("mem")
    mid_ref[:, :, lanes:] = jnp.zeros((quarters, rows, mid_ref.shape[2] - lanes), F32)
    for k in range(quarters):
        mid_ref[mine ^ k, :, :lanes] = piece_refs[k][...]
    whole = parts_ref[0]
    for q in range(1, quarters):
        whole = whole + parts_ref[q]
    whole_ref[...] = whole
    for f in range(2):
        low = lanes + f * span
        mid_ref[0, :, low + HALO : low + HALO + width] = whole_ref[:rows, f * width : (f + 1) * width]
        for b in range(4):
            block, lane = slice(16 * b, 16 * (b + 1)), 32 * b + 2 * HALO * f
            mid_ref[0, block, low : low + HALO] = whole_ref[rows:, lane : lane + HALO]
            mid_ref[0, block, low + HALO + width : low + span] = whole_ref[rows:, lane + HALO : lane + 2 * HALO]
    wide_ref[...] = jnp.zeros(wide_ref.shape, F32)
    cut_quarters(rate_ref[...], wide_ref, kept_ref, 0)
    cut_quarters(sea_ref[...].astype(F32), wide_ref, kept_ref, span)
    mid_ref[1, :, lanes : lanes + 2 * span] = kept_ref[mine, :, : 2 * span]
    out_ref[...] = jnp.zeros(out_ref.shape, F32)
    for edge, offset in ((0, HALO), (quarters - 1, span - 2 * HALO)):

        @pl.when(mine == edge)
        def _():
            for k, (q, lane) in enumerate(fields_of(quarters, lanes, span)):
                out_ref[:, k * HALO : (k + 1) * HALO] = mid_ref[q, :, lane + offset : lane + offset + HALO]


def fields_of(quarters, lanes, span):
    places = [(q, k) for q in range(quarters) for k in range(0, lanes, span)]
    return places + [(0, lanes), (0, lanes + span), (1, lanes), (1, lanes + span)]


def rim_kernel(mid_ref, got_ref, top_ref, bottom_ref, *, lanes, span):
    quarters, rows = mid_ref.shape[:2]
    mine = lax.axis_index("mem")
    for q in range(quarters):
        top_ref[q] = mid_ref[q, :HALO, :]
        bottom_ref[q] = mid_ref[q, rows - HALO :, :]
    for edge, offset in ((0, 0), (quarters - 1, span - HALO)):

        @pl.when(mine == edge)
        def _():
            for k, (q, lane) in enumerate(fields_of(quarters, lanes, span)):
                at, cut = slice(k * HALO, (k + 1) * HALO), slice(lane + offset, lane + offset + HALO)
                top_ref[q, :, cut] = got_ref[:HALO, at]
                bottom_ref[q, :, cut] = got_ref[rows - HALO :, at]


def product_kernel(
    mid_ref, north_ref, south_ref, got_ref, out_ref,
    members_ref, state_ref, weights_ref, tiled_ref, field_ref,
):
    groups, height, lanes = members_ref.shape
    rows = height - 2 * HALO
    width = out_ref.shape[2] // 2
    span = width + 2 * HALO
    windows = lanes // span
    divisor = groups * windows - 1
    pad = 8

    def tile_lanes(value):
        for k in range(windows):
            tiled_ref[:, k * span : (k + 1) * span] = value
        return tiled_ref[...]

    inner = slice(HALO, HALO + rows)
    for g in range(groups):
        for part_ref, at in ((north_ref, slice(0, HALO)), (mid_ref, inner), (south_ref, slice(HALO + rows, height))):
            members_ref[g, at, :] = part_ref[g, :, :lanes]
            if g < 2:
                for f in range(2):
                    low = lanes + f * span
                    field_ref[2 * g + f, at, :span] = part_ref[g, :, low : low + span]
    mine = lax.axis_index("mem")
    for edge, offset in ((0, 0), (lax.axis_size("mem") - 1, span - HALO)):

        @pl.when(mine == edge)
        def _():
            for k in range(groups * windows + 4):
                other = k - groups * windows
                ref = members_ref.at[k // windows] if other < 0 else field_ref.at[other]
                low = (k % windows * span if other < 0 else 0) + offset
                ref[inner, low : low + HALO] = got_ref[:, k * HALO : (k + 1) * HALO]

    lat = lax.axis_index("lat")
    for at, end in ((slice(0, HALO), 0), (slice(HALO + rows, height), lax.axis_size("lat") - 1)):
        field_ref[3, at, :span] = jnp.where(lat == end, 0.0, field_ref[3, at, :span])

    innovation = field_ref[0, :, :span]
    weight_sum = field_ref[1, :, :span]
    sea_cover = field_ref[3, :, :span]

    rate = tile_lanes(field_ref[2, :, :span])
    sea = tile_lanes(sea_cover)
    north = 0.5 * (rate + pltpu.roll(rate, height - 1, 0)) * sea * pltpu.roll(sea, height - 1, 0)
    east = 0.5 * (rate + pltpu.roll(rate, lanes - 1, 1)) * sea * pltpu.roll(sea, lanes - 1, 1)
    south = pltpu.roll(north, 1, 0)
    west = pltpu.roll(east, 1, 1)
    weights_ref[0] = 1.0 - (north + south + east + west)
    weights_ref[1] = north
    weights_ref[2] = south
    weights_ref[3] = east
    weights_ref[4] = west
    state_ref[...] = jnp.zeros(state_ref.shape, F32)

    def sweep(source, target):
        for r in range(0, height, 8):
            centre_w, north_w, south_w, east_w, west_w = (
                weights_ref[i, r : r + 8, :] for i in range(5)
            )
            for g in range(groups):
                centre = state_ref[source, g, pad + r : pad + r + 8, :]
                above = state_ref[source, g, pad + r + 1 : pad + r + 9, :]
                below = state_ref[source, g, pad + r - 1 : pad + r + 7, :]
                state_ref[target, g, pad + r : pad + r + 8, :] = (
                    centre_w * centre
                    + (north_w * above + south_w * below)
                    + (east_w * pltpu.roll(centre, lanes - 1, 1) + west_w * pltpu.roll(centre, 1, 1))
                )

    def covariance(source):
        tiled = tile_lanes(source)
        for g in range(groups):
            state_ref[0, g, pad : pad + height, :] = members_ref[g] * tiled

        def pair(_, carry):
            sweep(0, 1)
            sweep(1, 0)
            return carry

        lax.fori_loop(0, STEPS // 2, pair, 0)
        total = members_ref[0] * state_ref[0, 0, pad : pad + height, :]
        for g in range(1, groups):
            total = total + members_ref[g] * state_ref[0, g, pad : pad + height, :]
        tiled_ref[...] = total
        summed = tiled_ref[:, :span]
        for k in range(1, windows):
            summed = summed + tiled_ref[:, k * span : (k + 1) * span]
        return sea_cover * summed / divisor

    first_pass = covariance(innovation)
    increment = covariance(innovation - weight_sum * first_pass)
    field_ref[0, :, :span] = increment
    half = (height - 2 * HALO) // 2
    for q in range(out_ref.shape[0]):
        out_ref[q, :, :width] = field_ref[0, HALO : HALO + half, HALO : HALO + width]
        out_ref[q, :, width:] = field_ref[0, HALO + half : HALO + 2 * half, HALO : HALO + width]


def answer_kernel(pieces_ref, turned_ref, tile_ref, out_ref, reply_ref):
    quarters, half, width = pieces_ref.shape[0], pieces_ref.shape[1], pieces_ref.shape[2] // 2
    rows, cols = tile_ref.shape
    for q in range(quarters):
        tile_ref[:half, q * width : (q + 1) * width] = pieces_ref[q, :, :width]
        tile_ref[half:, q * width : (q + 1) * width] = pieces_ref[q, :, width:]
    high, low = halves(tile_ref[...])
    both = jnp.concatenate([high, low], axis=0).astype(BF16)
    lanes = turned_ref.shape[1]
    row_ids = lax.broadcasted_iota(I32, (rows, lanes), 0).astype(F32)
    col_ids = lax.broadcasted_iota(I32, (cols, lanes), 0).astype(F32)
    reply_ref[...] = jnp.zeros(reply_ref.shape, F32)
    for k in range(SLOTS):
        in_row = row_ids == turned_ref[2 * SLOTS + k : 2 * SLOTS + k + 1, :]
        in_col = col_ids == turned_ref[3 * SLOTS + k : 3 * SLOTS + k + 1, :]
        picked = jnp.dot(both, jnp.where(in_col, 1.0, 0.0).astype(BF16), preferred_element_type=F32)
        picked = picked[:rows] + picked[rows:]
        reply_ref[k : k + 1, :] = jnp.sum(jnp.where(in_row, picked, 0.0), axis=0, keepdims=True)
    out_ref[...] = reply_ref[...].T[:, :SLOTS]


def residual_kernel(owner_ref, rank_ref, depart_ref, got_ref, out_ref, wide_ref):
    places = got_ref.shape[0]
    chunks = owner_ref.shape[0]
    wide_ref[...] = jnp.zeros(wide_ref.shape, F32)
    wide_ref[:places, :SLOTS] = got_ref[...]
    turned = wide_ref[...].T[:SLOTS, :]
    high, low = halves(turned)
    both = jnp.concatenate([high, low], axis=0).astype(BF16)
    dest_ids = lax.broadcasted_iota(I32, (wide_ref.shape[0], LANES), 0)
    slot_ids = lax.broadcasted_iota(I32, (SLOTS, LANES), 0).astype(F32)
    for j in range(chunks):
        names = jnp.where(dest_ids == owner_ref[j : j + 1, :], 1.0, 0.0).astype(BF16)
        picked = jnp.dot(both, names, preferred_element_type=F32)
        picked = picked[:SLOTS] + picked[SLOTS:]
        value = jnp.sum(
            jnp.where(slot_ids == rank_ref[j : j + 1, :], picked, 0.0), axis=0, keepdims=True
        )
        out_ref[j : j + 1, :] = depart_ref[j : j + 1, :] - value


def shape(*dims, dtype=F32):
    return jax.ShapeDtypeStruct(dims, dtype)


def shift(first, last, axis):
    size = lax.axis_size(axis)
    up = [(i, (i + 1) % size) for i in range(size)]
    return lax.ppermute(last, axis, up), lax.ppermute(first, axis, [(j, i) for i, j in up])


def per_device(perturbations, diffusivity, sea_mask, obs_owner, obs_cell, obs_depart, obs_weight):
    members, rows, cols = perturbations.shape
    quarters = lax.axis_size("mem")
    places = lax.axis_size("lat") * lax.axis_size("lon")
    width = cols // quarters
    span = width + 2 * HALO
    height = rows + 2 * HALO
    chunks = obs_cell.shape[0] // LANES
    owner, cell, depart, weight = (
        a.reshape(chunks, LANES) for a in (obs_owner, obs_cell, obs_depart, obs_weight)
    )
    tiles = ("lat", "lon")

    lanes = members * span
    piece = shape(rows, lanes)
    pair = shape(2, rows, lanes)
    wide = pltpu.VMEM((rows, cols + LANES), F32)
    own, near, far = call(
        quarter_kernel, (piece, piece, pair), [pltpu.VMEM((quarters, rows, lanes), F32), wide]
    )(perturbations)
    outgoing, rank = call(
        pack_kernel,
        (shape(places, LANES), shape(chunks, LANES)),
        [pltpu.VMEM((chunks, LANES), a.dtype) for a in (owner, cell, depart, weight)]
        + [pltpu.SemaphoreType.DMA((4,))],
        place=AWAY,
    )(owner, cell, depart, weight)
    got = lax.all_to_all(outgoing, tiles, split_axis=0, concat_axis=0, tiled=True)
    far = lax.ppermute(far, "mem", [(i, i ^ 2) for i in range(quarters)])
    got, far = lax.optimization_barrier((got, far))

    parts, turned, passed = call(
        scatter_kernel,
        (shape(quarters, rows + 2 * HALO, 2 * width), shape(LANES, places), pair),
        [pltpu.VMEM((2, rows, cols + LANES), F32)],
    )(got, near, far)
    near = lax.ppermute(passed, "mem", [(i, i ^ 1) for i in range(quarters)])
    parts = lax.all_to_all(parts, "mem", split_axis=0, concat_axis=0, tiled=True)
    field_lanes = lanes + 2 * LANES
    strip = shape(quarters, HALO, field_lanes)
    rim_lanes = -(-(quarters * members + 4) * HALO // LANES) * LANES
    mid, edge = call(
        reduce_kernel,
        (shape(quarters, rows, field_lanes), shape(rows, rim_lanes)),
        [
            pltpu.VMEM((quarters, rows, 2 * LANES), F32),
            wide,
            pltpu.VMEM((rows + 2 * HALO, 2 * width), F32),
        ],
    )(parts, diffusivity, sea_mask, own, far, near)
    devices = lax.axis_size("lon") * quarters
    ends = [(i - 1, i % devices) for i in range(quarters, devices + 1, quarters)]
    got = lax.ppermute(edge, ("lon", "mem"), ends + [(j, i) for i, j in ends])
    top, bottom = call(functools.partial(rim_kernel, lanes=lanes, span=span), (strip, strip))(mid, got)
    north, south = shift(top, bottom, "lat")
    quarter = call(
        product_kernel,
        shape(quarters, rows // 2, 2 * width),
        [
            pltpu.VMEM((quarters, height, lanes), F32),
            pltpu.VMEM((2, quarters, height + 16, lanes), F32),
            pltpu.VMEM((5, height, lanes), F32),
            pltpu.VMEM((height, lanes), F32),
            pltpu.VMEM((4, height, LANES), F32),
        ],
    )(mid, north, south, got)
    quarter = lax.all_to_all(quarter, "mem", split_axis=0, concat_axis=0, tiled=True)
    increment, answers = call(
        answer_kernel, (shape(rows, cols), shape(places, SLOTS)), [pltpu.VMEM((LANES, places), F32)]
    )(quarter, turned)
    returned = lax.all_to_all(answers, tiles, split_axis=0, concat_axis=0, tiled=True)
    residual = call(
        residual_kernel, shape(chunks, LANES), [pltpu.VMEM((max(LANES, places), LANES), F32)]
    )(owner, rank, depart, returned)
    return increment, residual.reshape(chunks * LANES)


def solution(mesh):
    return jax.shard_map(
        per_device,
        mesh=mesh,
        in_specs=(
            P("mem", "lat", "lon"),
            P("lat", "lon"),
            P("lat", "lon"),
            P(("lat", "lon", "mem"), None),
            P(("lat", "lon", "mem")),
            P(("lat", "lon", "mem")),
            P(("lat", "lon", "mem")),
        ),
        out_specs=(P("lat", "lon"), P(("lat", "lon", "mem"))),
        check_vma=False,
    )
```
